512 devices in a mesh: ep: 32 (over x, y), node: 2 (over core), dp: 8 (over z).
Axes of the slice: x: 4, y: 8, z: 8, core: 2. Of those that a mesh axis runs over, the one named last changes fastest.
Arguments:
- grad_out: bfloat16 [8192, 7168], P(('ep', 'node'), 'dp'), may hold values from -6 to 6
- tokens: bfloat16 [8192, 7168], P(('ep', 'node'), 'dp'), may hold values from -0.59765625 to 0.59765625
- scores: float32 [8192, 64], P(('ep', 'node')), may hold values from 0.02 to 0.98
- expert_ids: int32 [8192, 8], P(('ep', 'node')), may hold values from 0 to 63, all different within a row; in each aligned block of 128 rows (0 to 127, 128 to 255, ...) at most 20 rows name the same one
- hidden_act: bfloat16 [64, 1280, 1024], P(('ep', 'node')), may hold values from -0.29882812 to 0.29882812
- down_weight: bfloat16 [64, 1024, 7168], P(('ep', 'node'), None, 'dp'), may hold values from -0.1875 to 0.1875
Outputs:
- weight_grad: bfloat16 [64, 1024, 7168], P(('ep', 'node'), None, 'dp')
- hidden_grad: bfloat16 [64, 1280, 1024], P(('ep', 'node'), 'dp')
- gate_grad: float32 [64, 7168], P(None, 'dp')
The draws below stay inside these ranges and needn't reach their ends.
Inputs may be any that keep to these rules, and one draw needn't show every extreme that they name: `expert_ids`: among the routes of the 128 tokens of one source device, no expert is named more than 20 times, a bound that some block reaches.
All inputs are finite; a program needn't handle non-finite values.
Results may differ from the reference program's by a relative error of at most 0.017.
Values may be sent and summed in bfloat16 or wider, within the bound.
No kernel may reach another device: no remote copies, remote signals or barrier semaphores. Data moves between devices by JAX's collectives and lax.ppermute only.
A program may use at most 64 MiB of HBM per device.

```python
import math
import jax
import jax.numpy as jnp
import numpy as np
from jax import lax

D = 7168
F = 1024
TOPK = 8
TOK_DEV = 128
EXPERTS = 64
MOST = 20
SLOTS = 1280
TOKENS = 8192
N_DP = 8


def levels(rng, extent, split, low, largest):
    def one(position, blocks):
        steps = jax.random.uniform(jax.random.fold_in(jax.random.fold_in(rng, 6), position), (blocks,), jnp.float32, low / len(split), largest / len(split))
        return jnp.repeat(jnp.exp(steps), extent[position] // blocks).reshape((-1,) + (1,) * (len(extent) - position - 1))

    gain = one(*split[0])
    for cut in split[1:]:
        gain = gain * one(*cut)
    return gain


def deal_out(own_key, own, number, rows, number_of, top, limit, slope):
    sequence = jax.random.permutation(own_key, number_of)
    packed, common = portions_of(number_of, rows * top, limit, slope, True), portions_of(number_of, rows * top, limit, slope, False)
    places = jnp.arange(number_of)

    def named(sizes, offset_by):
        used = int((sizes > 0).sum())
        fixed = max(1, used // 4)
        passed = fixed + (places - fixed + offset_by * (used - fixed)) % max(1, number_of - fixed)
        return jnp.zeros((number_of,), jnp.int32).at[sequence[jnp.where(places < fixed, places, passed)]].set(jnp.asarray(sizes, jnp.int32))

    sizes = jnp.where(number % 4 == 0, named(packed, number // 4), named(common, number - number // 4 - 1))
    mixed = jax.random.permutation(jax.random.fold_in(own, 3), number_of)
    donor, taker = mixed[0:number_of // 2 * 2:2], mixed[1:number_of // 2 * 2:2]
    room = jnp.minimum(sizes[donor] - 1, limit - sizes[taker]) // 2
    room = jnp.where((donor == sequence[0]) | (taker == sequence[0]) | (sizes[taker] == 0), 0, jnp.maximum(room, 0))
    passed = jax.random.randint(jax.random.fold_in(own, 4), (number_of // 2,), 0, 1 << 20) % (room + 1)
    sizes = sizes.at[donor].add(-passed).at[taker].add(passed)
    labels = jnp.searchsorted(jnp.cumsum(sizes), jnp.arange(rows * top), side="right").astype(jnp.int32)
    listing = labels.reshape(top, rows).T
    listing = listing[jax.random.permutation(jax.random.fold_in(own, 1), rows)]
    offset_by = jax.random.randint(jax.random.fold_in(own, 2), (rows, 1), 0, top)
    return jnp.take_along_axis(listing, (jnp.arange(top)[None, :] + offset_by) % top, axis=1)


def portions_of(count, total, bound, slope, full):
    portions = [(1 << 20) // math.isqrt(rank ** slope) + 1 for rank in range(1, count + 1)]
    largest = bound if full else min(bound, max(-(-total // count), total * portions[0] // sum(portions)))
    least = 1 if total - largest >= count - 1 else 0
    counts, rest = [largest] + [least] * (count - 1), total - largest - least * (count - 1)
    while rest > 0:
        movable = [i for i in range(1, count) if counts[i] < largest] or [i for i in range(1, count) if counts[i] < bound]
        whole, remaining = sum([portions[i] for i in movable]), rest
        for i in movable:
            extra = min(bound - counts[i], max(1, remaining * portions[i] // whole), rest)
            counts[i] = counts[i] + extra
            rest = rest - extra
    return np.array(counts)


def centred(own_key, dims, scale, limit, split=(), held_as=jnp.bfloat16):
    loudness = levels(own_key, dims, split, -0.22, 0.18) if split else 1.0
    array = jax.random.normal(own_key, dims, jnp.float32) * scale * loudness
    return jnp.minimum(jnp.maximum(array, -limit), limit).astype(held_as)


def setup_inputs(seed: int = 0) -> dict:
    arg_keys = jax.random.split(jax.random.key(seed), 7)
    grad_out = centred(arg_keys[0], (TOKENS, D), 1.0, 6.0, ((0, 64), (1, 8)))
    tokens = centred(arg_keys[1], (TOKENS, D), 0.1, 0.59765625, ((0, 64), (1, 8)))
    scores = jnp.clip(0.02 + 0.96000002 * jax.random.uniform(arg_keys[2], (TOKENS, EXPERTS), jnp.float32) ** levels(arg_keys[2], (TOKENS, EXPERTS), ((0, 64),), -0.2, 0.2), 0.02, 0.98)
    expert_ids_keys = jax.random.split(jax.random.fold_in(arg_keys[3], 1), TOKENS // TOK_DEV)
    expert_ids_turns = jax.random.permutation(jax.random.fold_in(arg_keys[3], 3), TOKENS // TOK_DEV)
    expert_ids = jax.vmap(lambda own, number: deal_out(jax.random.fold_in(arg_keys[3], 2), own, number, TOK_DEV, EXPERTS, TOPK, MOST, 2))(expert_ids_keys, expert_ids_turns).reshape((TOKENS, TOPK))
    hidden_act = centred(arg_keys[4], (EXPERTS, SLOTS, F), 0.05, 0.29882812, ((0, 64),))
    down_weight = centred(arg_keys[5], (EXPERTS, F, D), F ** -0.5, 0.1875, ((0, 64), (2, 8)))
    return dict(grad_out=grad_out, tokens=tokens, scores=scores, expert_ids=expert_ids, hidden_act=hidden_act, down_weight=down_weight)


route_scale = 2.5


def reference(grad_out, tokens, scores, expert_ids, hidden_act, down_weight):
    chosen = jnp.take_along_axis(scores, expert_ids, axis=1)
    total = jnp.sum(chosen, axis=1, keepdims=True)
    weights = (route_scale * chosen / total).astype(jnp.bfloat16)
    flat_ids = expert_ids.reshape(EXPERTS, TOK_DEV * TOPK)
    onehot = (flat_ids[:, :, None] == jnp.arange(EXPERTS, dtype=jnp.int32)[None, None, :]).astype(jnp.int32)
    before = jnp.cumsum(onehot, axis=1) - onehot
    rank = jnp.sum(before * onehot, axis=2)
    source = jnp.arange(EXPERTS, dtype=jnp.int32)[:, None]
    target = (flat_ids * SLOTS + source * MOST + rank).reshape(TOKENS * TOPK).astype(jnp.int32)
    route_index = jnp.arange(TOKENS * TOPK, dtype=jnp.int32)
    owner = jnp.full((EXPERTS * SLOTS,), -1, jnp.int32).at[target].set(route_index)
    owner = owner.reshape(EXPERTS, SLOTS)
    flat_weights = weights.reshape(TOKENS * TOPK)
    block_cols = D // N_DP

    def per_expert(operands):
        rows_of, hidden, down = operands
        valid = rows_of >= 0
        safe_rows = jnp.where(valid, rows_of, 0).astype(jnp.int32)
        rows = jnp.where(valid[:, None], grad_out[safe_rows // TOPK], jnp.zeros((), grad_out.dtype))
        gains = jnp.where(valid, flat_weights[safe_rows], jnp.zeros((), flat_weights.dtype))
        scaled = (gains.astype(jnp.float32)[:, None] * rows.astype(jnp.float32)).astype(jnp.bfloat16)
        weight_grad = lax.dot_general(hidden, scaled, (((0,), (0,)), ((), ())), preferred_element_type=jnp.float32).astype(jnp.bfloat16)
        outputs = jnp.dot(hidden, down, preferred_element_type=jnp.float32)
        slot_grad = jnp.sum(outputs * rows.astype(jnp.float32), axis=1)
        scaled_blocks = scaled.astype(jnp.float32).reshape(SLOTS, N_DP, block_cols)
        down_blocks = down.astype(jnp.float32).reshape(F, N_DP, block_cols)
        partials = jnp.einsum("snd,fnd->nsf", scaled_blocks, down_blocks, precision=lax.Precision.HIGHEST)
        rounded = lax.optimization_barrier(partials.astype(jnp.bfloat16))
        hidden_grad = jnp.sum(rounded.astype(jnp.float32), axis=0).astype(jnp.bfloat16)
        return weight_grad, hidden_grad, slot_grad

    weight_grad, hidden_grad, slot_grad = lax.map(per_expert, (owner, hidden_act, down_weight))
    route_grad = slot_grad.reshape(EXPERTS * SLOTS)[target].reshape(TOKENS, TOPK)
    mixed = jnp.sum(route_grad * chosen, axis=1, keepdims=True) / total
    score_grad = route_scale / total * (route_grad - mixed)
    logit_sel = score_grad * chosen * (1.0 - chosen)
    onehot_k = (expert_ids[:, :, None] == jnp.arange(EXPERTS, dtype=jnp.int32)[None, None, :]).astype(jnp.float32)
    logit_grad = jnp.sum(logit_sel[:, :, None] * onehot_k, axis=1).astype(jnp.bfloat16)
    gate_grad = jnp.dot(logit_grad.T, tokens, preferred_element_type=jnp.float32)
    return weight_grad, hidden_grad, gate_grad
```

```python
import functools

import jax
import jax.numpy as jnp
from jax import lax
from jax.experimental import pallas as pl
from jax.experimental.pallas import tpu as pltpu
from jax.sharding import PartitionSpec as P

route_scale = 2.5
TOKS = 128
TOP = 8
EXP = 64
MOST = 20
MAIN = 16
EXTRA = MOST - MAIN
FEAT = 896
LANES = 128
COLS = FEAT // LANES
PIECE = COLS * MAIN + 32
HID = 1024
SLOTS = EXP * MOST
GROUPS = 8
BLOCK = SLOTS // GROUPS
VMEM = 48 * 1024 * 1024
bf16, f32 = jnp.bfloat16, jnp.float32


def routing(ids, scores):
    expert = lax.broadcasted_iota(jnp.int32, (EXP, TOKS), 0)
    hit = ids[0:1, :] == expert
    for k in range(1, TOP):
        hit = hit | (ids[k : k + 1, :] == expert)
    earlier = (
        lax.broadcasted_iota(jnp.int32, (TOKS, TOKS), 0) < lax.broadcasted_iota(jnp.int32, (TOKS, TOKS), 1)
    )
    ones = jnp.where(hit, 1.0, 0.0)
    rank = jnp.dot(
        ones.astype(bf16), jnp.where(earlier, 1.0, 0.0).astype(bf16), preferred_element_type=f32
    )
    rank = jnp.where(hit, rank, -1.0)
    chosen = jnp.where(hit, scores, 0.0)
    total = jnp.sum(chosen, axis=0, keepdims=True)
    weights = (route_scale * chosen / total).astype(bf16).astype(f32)
    return hit, chosen, total, weights, rank


def pack_kernel(ids_ref, scores_ref, grad_ref, send_ref, rank_ref, weight_ref):
    _, _, _, weights, rank = routing(ids_ref[...], scores_ref[...])
    rank_ref[...] = rank
    weight_ref[...] = weights
    grad = grad_ref[...]
    row = lax.broadcasted_iota(jnp.int32, (8, MAIN, TOKS), 1)
    main_rank = row.astype(f32)
    extra_rank = (MAIN + row % EXTRA).astype(f32)
    quarter = lax.broadcasted_iota(jnp.int32, (8 * MAIN, LANES), 0) % MAIN // EXTRA

    def step(i, carry):
        at = pl.ds(pl.multiple_of(i * 8, 8), 8)
        ranks = rank_ref[at, :][:, None, :]
        gains = weight_ref[at, :][:, None, :]
        place = jnp.where(ranks == main_rank, gains, 0.0).reshape(8 * MAIN, TOKS).astype(bf16)
        rows = jnp.dot(place, grad, preferred_element_type=f32)
        for j in range(COLS):
            send_ref[at, MAIN * j : MAIN * (j + 1), :] = (
                rows[:, LANES * j : LANES * (j + 1)].astype(bf16).reshape(8, MAIN, LANES)
            )
        place = jnp.where(ranks == extra_rank, gains, 0.0).reshape(8 * MAIN, TOKS).astype(bf16)
        rows = jnp.dot(place, grad, preferred_element_type=f32)
        for part in range(2):
            mixed = jnp.zeros((8 * MAIN, LANES), f32)
            for q in range(4):
                j = part * 4 + q
                if j < COLS:
                    mixed = jnp.where(quarter == q, rows[:, LANES * j : LANES * (j + 1)], mixed)
            start = COLS * MAIN + part * MAIN
            send_ref[at, start : start + MAIN, :] = mixed.astype(bf16).reshape(8, MAIN, LANES)
        return carry

    lax.fori_loop(0, EXP // 8, step, 0)


def pack(ids, scores, grad):
    return pl.pallas_call(
        pack_kernel,
        out_shape=jax.ShapeDtypeStruct((EXP, PIECE, LANES), bf16),
        scratch_shapes=[pltpu.VMEM((EXP, TOKS), f32), pltpu.VMEM((EXP, TOKS), f32)],
        compiler_params=pltpu.CompilerParams(vmem_limit_bytes=VMEM),
        cost_estimate=pl.CostEstimate(flops=500_000_000, bytes_accessed=2_700_000, transcendentals=0),
    )(ids, scores, grad)


def order_kernel(x_ref, main_ref, extra_ref):
    i = lax.broadcasted_iota(jnp.int32, (BLOCK, BLOCK), 0)
    j = lax.broadcasted_iota(jnp.int32, (BLOCK, BLOCK), 1)
    e = i - 8 * MAIN
    origin = jnp.where(i < 8 * MAIN, i // MAIN * MOST + i % MAIN, e // EXTRA * MOST + MAIN + e % EXTRA)
    move = jnp.where(origin == j, 1.0, 0.0).astype(bf16)
    y = jnp.dot(move, x_ref[...], preferred_element_type=f32).astype(bf16)
    main_ref[...] = y[: 8 * MAIN]
    extra_ref[...] = y[8 * MAIN :]


def order(hidden):
    return pl.pallas_call(
        order_kernel,
        grid=(GROUPS,),
        in_specs=[pl.BlockSpec((BLOCK, HID), lambda i: (i, 0))],
        out_specs=[
            pl.BlockSpec((8 * MAIN, HID), lambda i: (i, 0)),
            pl.BlockSpec((8 * EXTRA, HID), lambda i: (i, 0)),
        ],
        out_shape=[
            jax.ShapeDtypeStruct((EXP * MAIN, HID), bf16),
            jax.ShapeDtypeStruct((EXP * EXTRA, HID), bf16),
        ],
        cost_estimate=pl.CostEstimate(flops=500_000_000, bytes_accessed=5_300_000, transcendentals=0),
    )(hidden)


def restore_kernel(x_ref, y_ref):
    j = lax.broadcasted_iota(jnp.int32, (BLOCK, BLOCK), 0)
    i = lax.broadcasted_iota(jnp.int32, (BLOCK, BLOCK), 1)
    e = i - 8 * MAIN
    origin = jnp.where(i < 8 * MAIN, i // MAIN * MOST + i % MAIN, e // EXTRA * MOST + MAIN + e % EXTRA)
    move = jnp.where(origin == j, 1.0, 0.0).astype(bf16)
    y_ref[...] = jnp.dot(move, x_ref[...], preferred_element_type=f32).astype(bf16)


def restore(x):
    return pl.pallas_call(
        restore_kernel,
        out_shape=jax.ShapeDtypeStruct((BLOCK, HID), bf16),
        cost_estimate=pl.CostEstimate(flops=60_000_000, bytes_accessed=660_000, transcendentals=0),
    )(x)


FBLOCK = 256


def expert_kernel(recv_ref, main_ref, extra_ref, down_ref, part_ref, slot_ref, rows_ref, acc_ref):
    step = pl.program_id(0)

    @pl.when(step == 0)
    def _():
        i = lax.broadcasted_iota(jnp.int32, (LANES, LANES), 0)
        j = lax.broadcasted_iota(jnp.int32, (LANES, LANES), 1)
        q, source, r = i // 32, i % 32 // EXTRA, i % EXTRA
        move = jnp.where(source * MAIN + q * EXTRA + r == j, 1.0, 0.0).astype(bf16)
        for g in range(GROUPS):
            at = slice(8 * g, 8 * g + 8)
            for j in range(COLS):
                rows_ref[LANES * g : LANES * (g + 1), LANES * j : LANES * (j + 1)] = recv_ref[
                    at, MAIN * j : MAIN * (j + 1), :
                ].reshape(LANES, LANES)
            for part in range(2):
                start = COLS * MAIN + part * MAIN
                x = recv_ref[at, start : start + MAIN, :].reshape(LANES, LANES)
                y = jnp.dot(move, x, preferred_element_type=f32).astype(bf16)
                for q in range(4):
                    j = part * 4 + q
                    if j < COLS:
                        rows_ref[
                            EXP * MAIN + 32 * g : EXP * MAIN + 32 * (g + 1), LANES * j : LANES * (j + 1)
                        ] = y[32 * q : 32 * (q + 1)]
        acc_ref[...] = jnp.zeros_like(acc_ref)

    chunk = 256
    for c in range(SLOTS // chunk):
        at = slice(c * chunk, (c + 1) * chunk)
        part = jnp.dot(rows_ref[at, :], down_ref[...], preferred_element_type=f32)
        if c < EXP * MAIN // chunk:
            hidden = main_ref[at, :]
        else:
            hidden = extra_ref[...]
        both = part * hidden.astype(f32)
        acc_ref[at, :] += both[:, :LANES] + both[:, LANES:]
        part = part.astype(bf16)
        if c < EXP * MAIN // chunk:
            for h in range(2):
                g = 2 * c + h
                part_ref[BLOCK * g : BLOCK * g + LANES, :] = part[LANES * h : LANES * (h + 1)]
        else:
            for g in range(GROUPS):
                part_ref[BLOCK * g + LANES : BLOCK * (g + 1), :] = part[32 * g : 32 * (g + 1)]

    @pl.when(step == pl.num_programs(0) - 1)
    def _():
        slot_ref[...] = lax.dot_general(
            jnp.ones((8, LANES), f32),
            acc_ref[...],
            (((1,), (1,)), ((), ())),
            precision=lax.Precision.HIGHEST,
            preferred_element_type=f32,
        )


def expert(recv, main, extra, down_t):
    return pl.pallas_call(
        expert_kernel,
        grid=(HID // FBLOCK,),
        in_specs=[
            pl.BlockSpec((EXP, PIECE, LANES), lambda i: (0, 0, 0)),
            pl.BlockSpec((EXP * MAIN, FBLOCK), lambda i: (0, i)),
            pl.BlockSpec((EXP * EXTRA, FBLOCK), lambda i: (0, i)),
            pl.BlockSpec((FEAT, FBLOCK), lambda i: (0, i)),
        ],
        out_specs=[
            pl.BlockSpec((SLOTS, FBLOCK), lambda i: (0, i)),
            pl.BlockSpec((8, SLOTS), lambda i: (0, 0)),
            pl.BlockSpec((SLOTS, FEAT), lambda i: (0, 0)),
        ],
        out_shape=[
            jax.ShapeDtypeStruct((SLOTS, HID), bf16),
            jax.ShapeDtypeStruct((8, SLOTS), f32),
            jax.ShapeDtypeStruct((SLOTS, FEAT), bf16),
        ],
        scratch_shapes=[pltpu.VMEM((SLOTS, LANES), f32)],
        compiler_params=pltpu.CompilerParams(vmem_limit_bytes=VMEM),
        cost_estimate=pl.CostEstimate(flops=2_400_000_000, bytes_accessed=11_000_000, transcendentals=0),
    )(recv, main, extra, down_t)


def spread_kernel(slot_ref, out_ref):
    summed = jnp.sum(slot_ref[...], axis=0, keepdims=True)
    for g in range(GROUPS):
        out_ref[8 * g : 8 * g + 8, :LANES] = jnp.broadcast_to(
            summed[:, LANES * g : LANES * (g + 1)], (8, LANES)
        )
        start = EXP * MAIN + LANES * (g // 4)
        out_ref[8 * g : 8 * g + 8, LANES:] = jnp.broadcast_to(summed[:, start : start + LANES], (8, LANES))


def spread(slot):
    return pl.pallas_call(
        spread_kernel,
        out_shape=jax.ShapeDtypeStruct((EXP, 2 * LANES), f32),
        cost_estimate=pl.CostEstimate(flops=10_000, bytes_accessed=110_000, transcendentals=0),
    )(slot)


def gate_kernel(shift_ref, ids_ref, scores_ref, back_ref, tokens_ref, out_ref):
    hit, chosen, total, weights, rank = routing(ids_ref[...], scores_ref[...])
    main = pltpu.roll(back_ref[:, :LANES], shift_ref[0], 1)
    extra = pltpu.roll(back_ref[:, LANES:], shift_ref[1], 1)
    route = jnp.zeros((EXP, TOKS), f32)
    for r in range(MOST):
        value = main[:, r : r + 1] if r < MAIN else extra[:, r - MAIN : r - MAIN + 1]
        route = route + jnp.where(rank == float(r), value, 0.0)
    route = jnp.where(hit, route / jnp.where(hit, weights, 1.0), 0.0)
    mixed = jnp.sum(route * chosen, axis=0, keepdims=True) / total
    score = route_scale / total * (route - mixed)
    logit = (score * chosen * (1.0 - chosen)).astype(bf16)
    out_ref[...] = jnp.dot(logit, tokens_ref[...], preferred_element_type=f32)


def gate(shifts, ids, scores, back, tokens):
    return pl.pallas_call(
        gate_kernel,
        in_specs=[pl.BlockSpec(memory_space=pltpu.SMEM)] + [pl.BlockSpec(memory_space=pltpu.VMEM)] * 4,
        out_shape=jax.ShapeDtypeStruct((EXP, FEAT), f32),
        cost_estimate=pl.CostEstimate(flops=15_000_000, bytes_accessed=560_000, transcendentals=0),
    )(shifts, ids, scores, back, tokens)


def body(grad_out, tokens, scores, expert_ids, hidden_act, down_weight):
    both = ("ep", "node")
    exchange = functools.partial(lax.all_to_all, split_axis=0, concat_axis=0, tiled=True)
    source = lax.axis_index("ep") * lax.axis_size("node") + lax.axis_index("node")
    ids, scores = expert_ids.T, scores.T
    send = pack(ids, scores, grad_out)
    recv = exchange(send, both)
    main, extra = order(hidden_act[0])
    down_t = down_weight[0].T
    part, slot, rows = expert(recv, main, extra, down_t)
    slot = exchange(slot, "dp")
    part, slot = lax.optimization_barrier((part, slot))
    summed = lax.psum_scatter(part, "dp", scatter_dimension=0, tiled=True)
    back = exchange(spread(slot), both)
    weight_grad = lax.dot_general(
        jnp.concatenate([main, extra], axis=0),
        rows,
        (((0,), (0,)), ((), ())),
        preferred_element_type=f32,
    ).astype(bf16)[None]
    group, place = source // 8, source % 8
    shifts = jnp.stack([-MAIN * place % LANES, -(32 * (group % 4) + EXTRA * place) % LANES]).astype(jnp.int32)
    gate_part = gate(shifts, ids, scores, back, tokens)
    gate_rows = exchange(gate_part, both)
    gate_row = jnp.sum(gate_rows, axis=0, keepdims=True)
    gate_grad = exchange(jnp.broadcast_to(gate_row, (EXP, FEAT)), both)
    hidden_grad = restore(summed)[None]
    return (weight_grad, hidden_grad, gate_grad)


def solution(mesh):
    return jax.shard_map(
        body,
        mesh=mesh,
        in_specs=(
            P(("ep", "node"), "dp"),
            P(("ep", "node"), "dp"),
            P(("ep", "node"), None),
            P(("ep", "node"), None),
            P(("ep", "node"), None, None),
            P(("ep", "node"), None, "dp"),
        ),
        out_specs=(P(("ep", "node"), None, "dp"), P(("ep", "node"), "dp", None), P(None, "dp")),
        check_vma=False,
    )
```

```python
import functools

import jax
import jax.numpy as jnp
from jax import lax
from jax.experimental import pallas as pl
from jax.experimental.pallas import tpu as pltpu
from jax.sharding import PartitionSpec as P

route_scale = 2.5
TOKS = 128
TOP = 8
EXP = 64
MOST = 20
MAIN = 16
EXTRA = MOST - MAIN
FEAT = 896
LANES = 128
COLS = FEAT // LANES
PIECE = COLS * MAIN + 32
HID = 1024
SLOTS = EXP * MOST
GROUPS = 8
BLOCK = SLOTS // GROUPS
VMEM = 60 * 1024 * 1024
bf16, f32 = jnp.bfloat16, jnp.float32


def routing(ids, scores):
    expert = lax.broadcasted_iota(jnp.int32, (EXP, TOKS), 0)
    hit = ids[0:1, :] == expert
    for k in range(1, TOP):
        hit = hit | (ids[k : k + 1, :] == expert)
    earlier = (
        lax.broadcasted_iota(jnp.int32, (TOKS, TOKS), 0) < lax.broadcasted_iota(jnp.int32, (TOKS, TOKS), 1)
    )
    ones = jnp.where(hit, 1.0, 0.0)
    rank = jnp.dot(
        ones.astype(bf16), jnp.where(earlier, 1.0, 0.0).astype(bf16), preferred_element_type=f32
    )
    rank = jnp.where(hit, rank, -1.0)
    chosen = jnp.where(hit, scores, 0.0)
    total = jnp.sum(chosen, axis=0, keepdims=True)
    weights = (route_scale * chosen / total).astype(bf16).astype(f32)
    return hit, chosen, total, weights, rank


def pack_kernel(ids_any, scores_any, grad_any, send_ref, ids_ref, scores_ref, grad_ref, rank_ref, weight_ref, sems):
    copies = [
        pltpu.make_async_copy(ids_any, ids_ref, sems.at[0]),
        pltpu.make_async_copy(scores_any, scores_ref, sems.at[1]),
        pltpu.make_async_copy(grad_any, grad_ref, sems.at[2]),
    ]
    for copy in copies:
        copy.start()
    copies[0].wait()
    copies[1].wait()
    _, _, _, weights, rank = routing(ids_ref[...], scores_ref[...])
    rank_ref[...] = rank
    weight_ref[...] = weights
    copies[2].wait()
    grad = grad_ref[...]
    row = lax.broadcasted_iota(jnp.int32, (8, MAIN, TOKS), 1)
    main_rank = row.astype(f32)
    extra_rank = (MAIN + row % EXTRA).astype(f32)
    quarter = lax.broadcasted_iota(jnp.int32, (8 * MAIN, LANES), 0) % MAIN // EXTRA

    def step(i, carry):
        at = pl.ds(pl.multiple_of(i * 8, 8), 8)
        ranks = rank_ref[at, :][:, None, :]
        gains = weight_ref[at, :][:, None, :]
        place = jnp.where(ranks == main_rank, gains, 0.0).reshape(8 * MAIN, TOKS).astype(bf16)
        rows = jnp.dot(place, grad, preferred_element_type=f32)
        for j in range(COLS):
            send_ref[at, MAIN * j : MAIN * (j + 1), :] = (
                rows[:, LANES * j : LANES * (j + 1)].astype(bf16).reshape(8, MAIN, LANES)
            )
        place = jnp.where(ranks == extra_rank, gains, 0.0).reshape(8 * MAIN, TOKS).astype(bf16)
        rows = jnp.dot(place, grad, preferred_element_type=f32)
        for part in range(2):
            mixed = jnp.zeros((8 * MAIN, LANES), f32)
            for q in range(4):
                j = part * 4 + q
                if j < COLS:
                    mixed = jnp.where(quarter == q, rows[:, LANES * j : LANES * (j + 1)], mixed)
            start = COLS * MAIN + part * MAIN
            send_ref[at, start : start + MAIN, :] = mixed.astype(bf16).reshape(8, MAIN, LANES)
        return carry

    lax.fori_loop(0, EXP // 8, step, 0, unroll=UNROLL)


UNROLL = 8


def pack(ids, scores, grad):
    return pl.pallas_call(
        pack_kernel,
        in_specs=[pl.BlockSpec(memory_space=pl.ANY)] * 3,
        out_shape=jax.ShapeDtypeStruct((EXP, PIECE, LANES), bf16),
        scratch_shapes=[
            pltpu.VMEM((TOP, TOKS), jnp.int32),
            pltpu.VMEM((EXP, TOKS), f32),
            pltpu.VMEM((TOKS, FEAT), bf16),
            pltpu.VMEM((EXP, TOKS), f32),
            pltpu.VMEM((EXP, TOKS), f32),
            pltpu.SemaphoreType.DMA((3,)),
        ],
        compiler_params=pltpu.CompilerParams(vmem_limit_bytes=VMEM),
        cost_estimate=pl.CostEstimate(flops=500_000_000, bytes_accessed=2_700_000, transcendentals=0),
    )(ids, scores, grad)


def order_kernel(x_ref, main_ref, extra_ref):
    i = lax.broadcasted_iota(jnp.int32, (BLOCK, BLOCK), 0)
    j = lax.broadcasted_iota(jnp.int32, (BLOCK, BLOCK), 1)
    e = i - 8 * MAIN
    origin = jnp.where(i < 8 * MAIN, i // MAIN * MOST + i % MAIN, e // EXTRA * MOST + MAIN + e % EXTRA)
    move = jnp.where(origin == j, 1.0, 0.0).astype(bf16)
    y = jnp.dot(move, x_ref[...], preferred_element_type=f32).astype(bf16)
    main_ref[...] = y[: 8 * MAIN]
    extra_ref[...] = y[8 * MAIN :]


def order(hidden):
    return pl.pallas_call(
        order_kernel,
        grid=(GROUPS,),
        in_specs=[pl.BlockSpec((BLOCK, HID), lambda i: (i, 0))],
        out_specs=[
            pl.BlockSpec((8 * MAIN, HID), lambda i: (i, 0)),
            pl.BlockSpec((8 * EXTRA, HID), lambda i: (i, 0)),
        ],
        out_shape=[
            jax.ShapeDtypeStruct((EXP * MAIN, HID), bf16),
            jax.ShapeDtypeStruct((EXP * EXTRA, HID), bf16),
        ],
        cost_estimate=pl.CostEstimate(flops=500_000_000, bytes_accessed=5_300_000, transcendentals=0),
    )(hidden)


def restore_kernel(x_ref, y_ref):
    j = lax.broadcasted_iota(jnp.int32, (BLOCK, BLOCK), 0)
    i = lax.broadcasted_iota(jnp.int32, (BLOCK, BLOCK), 1)
    e = i - 8 * MAIN
    origin = jnp.where(i < 8 * MAIN, i // MAIN * MOST + i % MAIN, e // EXTRA * MOST + MAIN + e % EXTRA)
    move = jnp.where(origin == j, 1.0, 0.0).astype(bf16)
    y_ref[...] = jnp.dot(move, x_ref[...], preferred_element_type=f32).astype(bf16)


def restore(x):
    return pl.pallas_call(
        restore_kernel,
        out_shape=jax.ShapeDtypeStruct((BLOCK, HID), bf16),
        cost_estimate=pl.CostEstimate(flops=60_000_000, bytes_accessed=660_000, transcendentals=0),
    )(x)


FBLOCK = 512


def expert_kernel(recv_ref, main_ref, extra_ref, down_ref, part_ref, slot_ref, rows_any, rows_ref, acc_ref, sem):
    step = pl.program_id(0)
    keep = pltpu.make_async_copy(rows_ref, rows_any, sem)

    @pl.when(step == 0)
    def _():
        i = lax.broadcasted_iota(jnp.int32, (LANES, LANES), 0)
        j = lax.broadcasted_iota(jnp.int32, (LANES, LANES), 1)
        q, source, r = i // 32, i % 32 // EXTRA, i % EXTRA
        move = jnp.where(source * MAIN + q * EXTRA + r == j, 1.0, 0.0).astype(bf16)
        for g in range(GROUPS):
            at = slice(8 * g, 8 * g + 8)
            for j in range(COLS):
                rows_ref[LANES * g : LANES * (g + 1), LANES * j : LANES * (j + 1)] = recv_ref[
                    at, MAIN * j : MAIN * (j + 1), :
                ].reshape(LANES, LANES)
            for part in range(2):
                start = COLS * MAIN + part * MAIN
                x = recv_ref[at, start : start + MAIN, :].reshape(LANES, LANES)
                y = jnp.dot(move, x, preferred_element_type=f32).astype(bf16)
                for q in range(4):
                    j = part * 4 + q
                    if j < COLS:
                        rows_ref[
                            EXP * MAIN + 32 * g : EXP * MAIN + 32 * (g + 1), LANES * j : LANES * (j + 1)
                        ] = y[32 * q : 32 * (q + 1)]
        acc_ref[...] = jnp.zeros_like(acc_ref)
        keep.start()

    for c in range(SLOTS // CHUNK):
        at = slice(c * CHUNK, (c + 1) * CHUNK)
        part = jnp.dot(rows_ref[at, :], down_ref[...], preferred_element_type=f32)
        if c < EXP * MAIN // CHUNK:
            hidden = main_ref[at, :]
        else:
            hidden = extra_ref[...]
        both = part * hidden.astype(f32)
        acc_ref[at, :] += sum(both[:, LANES * q : LANES * (q + 1)] for q in range(FBLOCK // LANES))
        part = part.astype(bf16)
        if c < EXP * MAIN // CHUNK:
            for h in range(CHUNK // LANES):
                g = CHUNK // LANES * c + h
                part_ref[BLOCK * g : BLOCK * g + LANES, :] = part[LANES * h : LANES * (h + 1)]
        else:
            for g in range(GROUPS):
                part_ref[BLOCK * g + LANES : BLOCK * (g + 1), :] = part[32 * g : 32 * (g + 1)]

    @pl.when(step == pl.num_programs(0) - 1)
    def _():
        ones = jnp.ones((8, LANES), bf16)
        rest = acc_ref[...]
        sums = jnp.zeros((8, SLOTS), f32)
        for _ in range(3):
            term = rest.astype(bf16)
            rest = rest - term.astype(f32)
            sums = sums + lax.dot_general(
                ones, term, (((1,), (1,)), ((), ())), preferred_element_type=f32
            )
        for g in range(SLOTS // LANES):
            slot_ref[:, g, :] = sums[:, LANES * g : LANES * (g + 1)]
        keep.wait()


CHUNK = 256
SLOT_ROWS = 16


def expert(recv, main, extra, down_t):
    return pl.pallas_call(
        expert_kernel,
        grid=(HID // FBLOCK,),
        in_specs=[
            pl.BlockSpec((EXP, PIECE, LANES), lambda i: (0, 0, 0)),
            pl.BlockSpec((EXP * MAIN, FBLOCK), lambda i: (0, i)),
            pl.BlockSpec((EXP * EXTRA, FBLOCK), lambda i: (0, i)),
            pl.BlockSpec((FEAT, FBLOCK), lambda i: (0, i)),
        ],
        out_specs=[
            pl.BlockSpec((SLOTS, FBLOCK), lambda i: (0, i)),
            pl.BlockSpec((GROUPS, SLOT_ROWS, LANES), lambda i: (0, 0, 0)),
            pl.BlockSpec(memory_space=pl.ANY),
        ],
        out_shape=[
            jax.ShapeDtypeStruct((SLOTS, HID), bf16),
            jax.ShapeDtypeStruct((GROUPS, SLOT_ROWS, LANES), f32),
            jax.ShapeDtypeStruct((SLOTS, FEAT), bf16),
        ],
        scratch_shapes=[
            pltpu.VMEM((SLOTS, FEAT), bf16),
            pltpu.VMEM((SLOTS, LANES), f32),
            pltpu.SemaphoreType.DMA(()),
        ],
        compiler_params=pltpu.CompilerParams(vmem_limit_bytes=VMEM),
        cost_estimate=pl.CostEstimate(flops=2_400_000_000, bytes_accessed=11_000_000, transcendentals=0),
    )(recv, main, extra, down_t)


def spread_kernel(slot_ref, out_ref):
    summed = jnp.sum(slot_ref[...], axis=0)
    main = summed[:GROUPS]
    pairs = summed[GROUPS : GROUPS + 2]
    lane = lax.broadcasted_iota(jnp.int32, (GROUPS, LANES), 1)
    group = lax.broadcasted_iota(jnp.int32, (GROUPS, LANES), 0)
    extra = jnp.zeros((GROUPS, LANES), f32)
    for q in range(4):
        moved = pltpu.roll(pairs, (MAIN - 32 * q) % LANES, 1)
        for h in range(2):
            extra = jnp.where(group == 4 * h + q, moved[h : h + 1], extra)
    for place in range(8):
        a = pltpu.roll(main, -MAIN * place % LANES, 1) if place else main
        b = pltpu.roll(extra, -EXTRA * place % LANES, 1) if place else extra
        value = jnp.where(lane < MAIN, a, b)
        for g in range(GROUPS):
            out_ref[8 * g + place : 8 * g + place + 1, :] = value[g : g + 1]


def spread(slot):
    return pl.pallas_call(
        spread_kernel,
        out_shape=jax.ShapeDtypeStruct((EXP, LANES), f32),
        cost_estimate=pl.CostEstimate(flops=10_000, bytes_accessed=100_000, transcendentals=0),
    )(slot)


def gate_kernel(ids_ref, scores_ref, back_ref, tokens_ref, out_ref):
    hit, chosen, total, weights, rank = routing(ids_ref[...], scores_ref[...])
    route = jnp.zeros((EXP, TOKS), f32)
    for r in range(MOST):
        route = route + jnp.where(rank == float(r), back_ref[:, r : r + 1], 0.0)
    route = jnp.where(hit, route / jnp.where(hit, weights, 1.0), 0.0)
    mixed = jnp.sum(route * chosen, axis=0, keepdims=True) / total
    score = route_scale / total * (route - mixed)
    logit = (score * chosen * (1.0 - chosen)).astype(bf16)
    grad = jnp.dot(logit, tokens_ref[...], preferred_element_type=f32)
    for j in range(COLS):
        out_ref[:, j, :] = grad[:, LANES * j : LANES * (j + 1)]
    out_ref[:, COLS, :] = jnp.zeros((EXP, LANES), f32)


def gate(ids, scores, back, tokens):
    return pl.pallas_call(
        gate_kernel,
        out_shape=jax.ShapeDtypeStruct((EXP, COLS + 1, LANES), f32),
        cost_estimate=pl.CostEstimate(flops=15_000_000, bytes_accessed=560_000, transcendentals=0),
    )(ids, scores, back, tokens)


def total_kernel(x_ref, out_ref):
    out_ref[...] = jnp.broadcast_to(jnp.sum(x_ref[...], axis=0, keepdims=True), out_ref.shape)


def total_rows(x):
    return pl.pallas_call(
        total_kernel,
        out_shape=jax.ShapeDtypeStruct(x.shape, f32),
        cost_estimate=pl.CostEstimate(flops=66_000, bytes_accessed=520_000, transcendentals=0),
    )(x)


def flatten_kernel(x_ref, out_ref):
    for j in range(COLS):
        out_ref[:, LANES * j : LANES * (j + 1)] = x_ref[:, j, :]


def flatten(x):
    return pl.pallas_call(
        flatten_kernel,
        out_shape=jax.ShapeDtypeStruct((EXP, FEAT), f32),
        cost_estimate=pl.CostEstimate(flops=0, bytes_accessed=490_000, transcendentals=0),
    )(x)


def body(grad_out, tokens, scores, expert_ids, hidden_act, down_weight):
    both = ("ep", "node")
    exchange = functools.partial(lax.all_to_all, split_axis=0, concat_axis=0, tiled=True)
    ids, scores = expert_ids.T, scores.T
    recv = exchange(pack(ids, scores, grad_out), both)
    main, extra = order(hidden_act[0])
    part, slot, rows = expert(recv, main, extra, down_weight[0].T)
    slot = exchange(slot, "dp")
    part, slot = lax.optimization_barrier((part, slot))
    summed = lax.psum_scatter(part, "dp", scatter_dimension=0, tiled=True)
    back = exchange(spread(slot), both)
    weight_grad = lax.dot_general(
        jnp.concatenate([main, extra], axis=0),
        rows,
        (((0,), (0,)), ((), ())),
        preferred_element_type=f32,
    ).astype(bf16)[None]
    back, weight_grad = lax.optimization_barrier((back, weight_grad))
    gate_rows = exchange(gate(ids, scores, back, tokens), both)
    gate_grad = flatten(exchange(total_rows(gate_rows), both))
    hidden_grad = restore(summed)[None]
    return (weight_grad, hidden_grad, gate_grad)


def solution(mesh):
    return jax.shard_map(
        body,
        mesh=mesh,
        in_specs=(
            P(("ep", "node"), "dp"),
            P(("ep", "node"), "dp"),
            P(("ep", "node"), None),
            P(("ep", "node"), None),
            P(("ep", "node"), None, None),
            P(("ep", "node"), None, "dp"),
        ),
        out_specs=(P(("ep", "node"), None, "dp"), P(("ep", "node"), "dp", None), P(None, "dp")),
        check_vma=False,
    )
```

```python
import functools

import jax
import jax.numpy as jnp
from jax import lax
from jax.experimental import pallas as pl
from jax.experimental.pallas import tpu as pltpu
from jax.sharding import PartitionSpec as P

route_scale = 2.5
TOKS = 128
TOP = 8
EXP = 64
MOST = 20
MAIN = 16
EXTRA = MOST - MAIN
FEAT = 896
LANES = 128
COLS = FEAT // LANES
PIECE = COLS * MAIN + 32
HID = 1024
SLOTS = EXP * MOST
GROUPS = 8
BLOCK = SLOTS // GROUPS
MIB = 1024 * 1024
bf16, f32 = jnp.bfloat16, jnp.float32


def routing(ids, scores):
    expert = lax.broadcasted_iota(jnp.int32, (EXP, TOKS), 0)
    hit = ids[0:1, :] == expert
    for k in range(1, TOP):
        hit = hit | (ids[k : k + 1, :] == expert)
    earlier = (
        lax.broadcasted_iota(jnp.int32, (TOKS, TOKS), 0) < lax.broadcasted_iota(jnp.int32, (TOKS, TOKS), 1)
    )
    ones = jnp.where(hit, 1.0, 0.0)
    rank = jnp.dot(
        ones.astype(bf16), jnp.where(earlier, 1.0, 0.0).astype(bf16), preferred_element_type=f32
    )
    rank = jnp.where(hit, rank, -1.0)
    chosen = jnp.where(hit, scores, 0.0)
    total = jnp.sum(chosen, axis=0, keepdims=True)
    weights = (route_scale * chosen / total).astype(bf16).astype(f32)
    return hit, chosen, total, weights, rank


def pack_kernel(ids_any, scores_any, grad_any, send_ref, ids_ref, scores_ref, grad_ref, rank_ref, weight_ref, sems):
    copies = [
        pltpu.make_async_copy(ids_any, ids_ref, sems.at[0]),
        pltpu.make_async_copy(scores_any, scores_ref, sems.at[1]),
        pltpu.make_async_copy(grad_any, grad_ref, sems.at[2]),
    ]
    for copy in copies:
        copy.start()
    copies[0].wait()
    copies[1].wait()
    _, _, _, weights, rank = routing(ids_ref[...], scores_ref[...])
    rank_ref[...] = rank
    weight_ref[...] = weights
    copies[2].wait()
    grad = grad_ref[...]
    row = lax.broadcasted_iota(jnp.int32, (8, MAIN, TOKS), 1)
    main_rank = row.astype(f32)
    extra_rank = (MAIN + row % EXTRA).astype(f32)
    quarter = lax.broadcasted_iota(jnp.int32, (8 * MAIN, LANES), 0) % MAIN // EXTRA

    def step(i, carry):
        at = pl.ds(pl.multiple_of(i * 8, 8), 8)
        ranks = rank_ref[at, :][:, None, :]
        gains = weight_ref[at, :][:, None, :]
        place = jnp.where(ranks == main_rank, gains, 0.0).reshape(8 * MAIN, TOKS).astype(bf16)
        rows = jnp.dot(place, grad, preferred_element_type=f32)
        for j in range(COLS):
            send_ref[at, MAIN * j : MAIN * (j + 1), :] = (
                rows[:, LANES * j : LANES * (j + 1)].astype(bf16).reshape(8, MAIN, LANES)
            )
        place = jnp.where(ranks == extra_rank, gains, 0.0).reshape(8 * MAIN, TOKS).astype(bf16)
        rows = jnp.dot(place, grad, preferred_element_type=f32)
        for part in range(2):
            mixed = jnp.zeros((8 * MAIN, LANES), f32)
            for q in range(4):
                j = part * 4 + q
                if j < COLS:
                    mixed = jnp.where(quarter == q, rows[:, LANES * j : LANES * (j + 1)], mixed)
            start = COLS * MAIN + part * MAIN
            send_ref[at, start : start + MAIN, :] = mixed.astype(bf16).reshape(8, MAIN, LANES)
        return carry

    lax.fori_loop(0, EXP // 8, step, 0, unroll=UNROLL)


UNROLL = 8


def pack(ids, scores, grad):
    return pl.pallas_call(
        pack_kernel,
        in_specs=[pl.BlockSpec(memory_space=pl.ANY)] * 3,
        out_shape=jax.ShapeDtypeStruct((EXP, PIECE, LANES), bf16),
        scratch_shapes=[
            pltpu.VMEM((TOP, TOKS), jnp.int32),
            pltpu.VMEM((EXP, TOKS), f32),
            pltpu.VMEM((TOKS, FEAT), bf16),
            pltpu.VMEM((EXP, TOKS), f32),
            pltpu.VMEM((EXP, TOKS), f32),
            pltpu.SemaphoreType.DMA((3,)),
        ],
        compiler_params=pltpu.CompilerParams(vmem_limit_bytes=60 * MIB),
        cost_estimate=pl.CostEstimate(flops=500_000_000, bytes_accessed=2_700_000, transcendentals=0),
    )(ids, scores, grad)


def order_kernel(x_ref, main_ref, extra_ref):
    i = lax.broadcasted_iota(jnp.int32, (BLOCK, BLOCK), 0)
    j = lax.broadcasted_iota(jnp.int32, (BLOCK, BLOCK), 1)
    e = i - 8 * MAIN
    origin = jnp.where(i < 8 * MAIN, i // MAIN * MOST + i % MAIN, e // EXTRA * MOST + MAIN + e % EXTRA)
    move = jnp.where(origin == j, 1.0, 0.0).astype(bf16)
    y = jnp.dot(move, x_ref[...], preferred_element_type=f32).astype(bf16)
    main_ref[...] = y[: 8 * MAIN]
    extra_ref[...] = y[8 * MAIN :]


def order(hidden):
    return pl.pallas_call(
        order_kernel,
        grid=(GROUPS,),
        in_specs=[pl.BlockSpec((BLOCK, HID), lambda i: (i, 0))],
        out_specs=[
            pl.BlockSpec((8 * MAIN, HID), lambda i: (i, 0)),
            pl.BlockSpec((8 * EXTRA, HID), lambda i: (i, 0)),
        ],
        out_shape=[
            jax.ShapeDtypeStruct((EXP * MAIN, HID), bf16),
            jax.ShapeDtypeStruct((EXP * EXTRA, HID), bf16),
        ],
        cost_estimate=pl.CostEstimate(flops=500_000_000, bytes_accessed=5_300_000, transcendentals=0),
    )(hidden)


def restore_kernel(x_ref, y_ref):
    j = lax.broadcasted_iota(jnp.int32, (BLOCK, BLOCK), 0)
    i = lax.broadcasted_iota(jnp.int32, (BLOCK, BLOCK), 1)
    e = i - 8 * MAIN
    origin = jnp.where(i < 8 * MAIN, i // MAIN * MOST + i % MAIN, e // EXTRA * MOST + MAIN + e % EXTRA)
    move = jnp.where(origin == j, 1.0, 0.0).astype(bf16)
    y_ref[...] = jnp.dot(move, x_ref[...], preferred_element_type=f32).astype(bf16)


def restore(x):
    return pl.pallas_call(
        restore_kernel,
        out_shape=jax.ShapeDtypeStruct((BLOCK, HID), bf16),
        compiler_params=pltpu.CompilerParams(vmem_limit_bytes=4 * MIB),
        cost_estimate=pl.CostEstimate(flops=60_000_000, bytes_accessed=660_000, transcendentals=0),
    )(x)


FBLOCK = 512


def expert_kernel(recv_ref, main_ref, extra_ref, down_ref, part_ref, slot_ref, rows_any, rows_ref, acc_ref, sem):
    step = pl.program_id(0)
    keep = pltpu.make_async_copy(rows_ref, rows_any, sem)

    @pl.when(step == 0)
    def _():
        i = lax.broadcasted_iota(jnp.int32, (LANES, LANES), 0)
        j = lax.broadcasted_iota(jnp.int32, (LANES, LANES), 1)
        q, source, r = i // 32, i % 32 // EXTRA, i % EXTRA
        move = jnp.where(source * MAIN + q * EXTRA + r == j, 1.0, 0.0).astype(bf16)
        for g in range(GROUPS):
            at = slice(8 * g, 8 * g + 8)
            for j in range(COLS):
                rows_ref[LANES * g : LANES * (g + 1), LANES * j : LANES * (j + 1)] = recv_ref[
                    at, MAIN * j : MAIN * (j + 1), :
                ].reshape(LANES, LANES)
            for part in range(2):
                start = COLS * MAIN + part * MAIN
                x = recv_ref[at, start : start + MAIN, :].reshape(LANES, LANES)
                y = jnp.dot(move, x, preferred_element_type=f32).astype(bf16)
                for q in range(4):
                    j = part * 4 + q
                    if j < COLS:
                        rows_ref[
                            EXP * MAIN + 32 * g : EXP * MAIN + 32 * (g + 1), LANES * j : LANES * (j + 1)
                        ] = y[32 * q : 32 * (q + 1)]
        acc_ref[...] = jnp.zeros_like(acc_ref)
        keep.start()

    for c in range(SLOTS // CHUNK):
        at = slice(c * CHUNK, (c + 1) * CHUNK)
        part = jnp.dot(rows_ref[at, :], down_ref[...], preferred_element_type=f32)
        if c < EXP * MAIN // CHUNK:
            hidden = main_ref[at, :]
        else:
            hidden = extra_ref[...]
        both = part * hidden.astype(f32)
        acc_ref[at, :] += sum(both[:, LANES * q : LANES * (q + 1)] for q in range(FBLOCK // LANES))
        part = part.astype(bf16)
        if c < EXP * MAIN // CHUNK:
            for h in range(CHUNK // LANES):
                g = CHUNK // LANES * c + h
                part_ref[BLOCK * g : BLOCK * g + LANES, :] = part[LANES * h : LANES * (h + 1)]
        else:
            for g in range(GROUPS):
                part_ref[BLOCK * g + LANES : BLOCK * (g + 1), :] = part[32 * g : 32 * (g + 1)]

    @pl.when(step == pl.num_programs(0) - 1)
    def _():
        ones = jnp.ones((8, LANES), bf16)
        rest = acc_ref[...]
        sums = jnp.zeros((8, SLOTS), f32)
        for _ in range(3):
            term = rest.astype(bf16)
            rest = rest - term.astype(f32)
            sums = sums + lax.dot_general(
                ones, term, (((1,), (1,)), ((), ())), preferred_element_type=f32
            )
        for g in range(SLOTS // LANES):
            slot_ref[:, g, :] = sums[:, LANES * g : LANES * (g + 1)]
        keep.wait()


CHUNK = 256
SLOT_ROWS = 16


def expert(recv, main, extra, down_t):
    return pl.pallas_call(
        expert_kernel,
        grid=(HID // FBLOCK,),
        in_specs=[
            pl.BlockSpec((EXP, PIECE, LANES), lambda i: (0, 0, 0)),
            pl.BlockSpec((EXP * MAIN, FBLOCK), lambda i: (0, i)),
            pl.BlockSpec((EXP * EXTRA, FBLOCK), lambda i: (0, i)),
            pl.BlockSpec((FEAT, FBLOCK), lambda i: (0, i)),
        ],
        out_specs=[
            pl.BlockSpec((SLOTS, FBLOCK), lambda i: (0, i)),
            pl.BlockSpec((GROUPS, SLOT_ROWS, LANES), lambda i: (0, 0, 0)),
            pl.BlockSpec(memory_space=pl.ANY),
        ],
        out_shape=[
            jax.ShapeDtypeStruct((SLOTS, HID), bf16),
            jax.ShapeDtypeStruct((GROUPS, SLOT_ROWS, LANES), f32),
            jax.ShapeDtypeStruct((SLOTS, FEAT), bf16),
        ],
        scratch_shapes=[
            pltpu.VMEM((SLOTS, FEAT), bf16),
            pltpu.VMEM((SLOTS, LANES), f32),
            pltpu.SemaphoreType.DMA(()),
        ],
        compiler_params=pltpu.CompilerParams(vmem_limit_bytes=24 * MIB),
        cost_estimate=pl.CostEstimate(flops=2_400_000_000, bytes_accessed=11_000_000, transcendentals=0),
    )(recv, main, extra, down_t)


def spread_kernel(slot_ref, out_ref):
    summed = jnp.sum(slot_ref[...], axis=0)
    main = summed[:GROUPS]
    pairs = summed[GROUPS : GROUPS + 2]
    lane = lax.broadcasted_iota(jnp.int32, (GROUPS, LANES), 1)
    group = lax.broadcasted_iota(jnp.int32, (GROUPS, LANES), 0)
    extra = jnp.zeros((GROUPS, LANES), f32)
    for q in range(4):
        moved = pltpu.roll(pairs, (MAIN - 32 * q) % LANES, 1)
        for h in range(2):
            extra = jnp.where(group == 4 * h + q, moved[h : h + 1], extra)
    for place in range(8):
        a = pltpu.roll(main, -MAIN * place % LANES, 1) if place else main
        b = pltpu.roll(extra, -EXTRA * place % LANES, 1) if place else extra
        value = jnp.where(lane < MAIN, a, b)
        for g in range(GROUPS):
            out_ref[8 * g + place : 8 * g + place + 1, :] = value[g : g + 1]


def spread(slot):
    return pl.pallas_call(
        spread_kernel,
        out_shape=jax.ShapeDtypeStruct((EXP, LANES), f32),
        compiler_params=pltpu.CompilerParams(vmem_limit_bytes=2 * MIB),
        cost_estimate=pl.CostEstimate(flops=10_000, bytes_accessed=100_000, transcendentals=0),
    )(slot)


def gate_kernel(ids_ref, scores_ref, back_ref, tokens_ref, out_ref):
    hit, chosen, total, weights, rank = routing(ids_ref[...], scores_ref[...])
    route = jnp.zeros((EXP, TOKS), f32)
    for r in range(MOST):
        route = route + jnp.where(rank == float(r), back_ref[:, r : r + 1], 0.0)
    route = jnp.where(hit, route / jnp.where(hit, weights, 1.0), 0.0)
    mixed = jnp.sum(route * chosen, axis=0, keepdims=True) / total
    score = route_scale / total * (route - mixed)
    logit = (score * chosen * (1.0 - chosen)).astype(bf16)
    out_ref[...] = jnp.dot(logit, tokens_ref[...], preferred_element_type=f32)


def gate(ids, scores, back, tokens):
    return pl.pallas_call(
        gate_kernel,
        out_shape=jax.ShapeDtypeStruct((EXP, FEAT), f32),
        compiler_params=pltpu.CompilerParams(vmem_limit_bytes=4 * MIB),
        cost_estimate=pl.CostEstimate(flops=15_000_000, bytes_accessed=560_000, transcendentals=0),
    )(ids, scores, back, tokens)


def body(grad_out, tokens, scores, expert_ids, hidden_act, down_weight):
    both = ("ep", "node")
    exchange = functools.partial(lax.all_to_all, split_axis=0, concat_axis=0, tiled=True)
    ids, scores = expert_ids.T, scores.T
    recv = exchange(pack(ids, scores, grad_out), both)
    main, extra = order(hidden_act[0])
    part, slot, rows = expert(recv, main, extra, down_weight[0].T)
    slot = exchange(slot, "dp")
    summed = lax.psum_scatter(part, "dp", scatter_dimension=0, tiled=True)
    back = exchange(spread(slot), both)
    weight_grad = lax.dot_general(
        jnp.concatenate([main, extra], axis=0),
        rows,
        (((0,), (0,)), ((), ())),
        preferred_element_type=f32,
    ).astype(bf16)[None]
    back, weight_grad = lax.optimization_barrier((back, weight_grad))
    gate_rows = exchange(gate(ids, scores, back, tokens), both)
    gate_row = jnp.sum(gate_rows, axis=0, keepdims=True)
    gate_row, summed = lax.optimization_barrier((gate_row, summed))
    gate_grad = exchange(jnp.broadcast_to(gate_row, (EXP, FEAT)), both)
    hidden_grad = restore(summed)[None]
    return (weight_grad, hidden_grad, gate_grad)


def solution(mesh):
    return jax.shard_map(
        body,
        mesh=mesh,
        in_specs=(
            P(("ep", "node"), "dp"),
            P(("ep", "node"), "dp"),
            P(("ep", "node"), None),
            P(("ep", "node"), None),
            P(("ep", "node"), None, None),
            P(("ep", "node"), None, "dp"),
        ),
        out_specs=(P(("ep", "node"), None, "dp"), P(("ep", "node"), "dp", None), P(None, "dp")),
        check_vma=False,
    )
```

```python
import functools

import jax
import jax.numpy as jnp
from jax import lax
from jax.experimental import pallas as pl
from jax.experimental.pallas import tpu as pltpu
from jax.sharding import PartitionSpec as P

route_scale = 2.5
TOKS = 128
TOP = 8
EXP = 64
MOST = 20
MAIN = 16
EXTRA = MOST - MAIN
FEAT = 896
LANES = 128
COLS = FEAT // LANES
PIECE = COLS * MAIN + 32
HID = 1024
SLOTS = EXP * MOST
GROUPS = 8
BLOCK = SLOTS // GROUPS
MIB = 1024 * 1024
bf16, f32 = jnp.bfloat16, jnp.float32


def routing(ids, scores):
    expert = lax.broadcasted_iota(jnp.int32, (EXP, TOKS), 0)
    hit = ids[0:1, :] == expert
    for k in range(1, TOP):
        hit = hit | (ids[k : k + 1, :] == expert)
    earlier = (
        lax.broadcasted_iota(jnp.int32, (TOKS, TOKS), 0) < lax.broadcasted_iota(jnp.int32, (TOKS, TOKS), 1)
    )
    ones = jnp.where(hit, 1.0, 0.0)
    rank = jnp.dot(
        ones.astype(bf16), jnp.where(earlier, 1.0, 0.0).astype(bf16), preferred_element_type=f32
    )
    rank = jnp.where(hit, rank, -1.0)
    chosen = jnp.where(hit, scores, 0.0)
    total = jnp.sum(chosen, axis=0, keepdims=True)
    weights = (route_scale * chosen / total).astype(bf16).astype(f32)
    return hit, chosen, total, weights, rank


def pack_kernel(ids_any, scores_any, grad_any, send_ref, ids_ref, scores_ref, grad_ref, rank_ref, weight_ref, sems):
    copies = [
        pltpu.make_async_copy(ids_any, ids_ref, sems.at[0]),
        pltpu.make_async_copy(scores_any, scores_ref, sems.at[1]),
        pltpu.make_async_copy(grad_any, grad_ref, sems.at[2]),
    ]
    for copy in copies:
        copy.start()
    copies[0].wait()
    copies[1].wait()
    _, _, _, weights, rank = routing(ids_ref[...], scores_ref[...])
    rank_ref[...] = rank
    weight_ref[...] = weights
    copies[2].wait()
    grad = grad_ref[...]
    row = lax.broadcasted_iota(jnp.int32, (8, MAIN, TOKS), 1)
    main_rank = row.astype(f32)
    extra_rank = (MAIN + row % EXTRA).astype(f32)
    quarter = lax.broadcasted_iota(jnp.int32, (8 * MAIN, LANES), 0) % MAIN // EXTRA

    def step(i, carry):
        at = pl.ds(pl.multiple_of(i * 8, 8), 8)
        ranks = rank_ref[at, :][:, None, :]
        gains = weight_ref[at, :][:, None, :]
        place = jnp.where(ranks == main_rank, gains, 0.0).reshape(8 * MAIN, TOKS).astype(bf16)
        rows = jnp.dot(place, grad, preferred_element_type=f32)
        for j in range(COLS):
            send_ref[at, MAIN * j : MAIN * (j + 1), :] = (
                rows[:, LANES * j : LANES * (j + 1)].astype(bf16).reshape(8, MAIN, LANES)
            )
        place = jnp.where(ranks == extra_rank, gains, 0.0).reshape(8 * MAIN, TOKS).astype(bf16)
        rows = jnp.dot(place, grad, preferred_element_type=f32)
        for part in range(2):
            mixed = jnp.zeros((8 * MAIN, LANES), f32)
            for q in range(4):
                j = part * 4 + q
                if j < COLS:
                    mixed = jnp.where(quarter == q, rows[:, LANES * j : LANES * (j + 1)], mixed)
            start = COLS * MAIN + part * MAIN
            send_ref[at, start : start + MAIN, :] = mixed.astype(bf16).reshape(8, MAIN, LANES)
        return carry

    lax.fori_loop(0, EXP // 8, step, 0, unroll=UNROLL)


UNROLL = 8


def pack(ids, scores, grad):
    return pl.pallas_call(
        pack_kernel,
        in_specs=[pl.BlockSpec(memory_space=pl.ANY)] * 3,
        out_shape=jax.ShapeDtypeStruct((EXP, PIECE, LANES), bf16),
        scratch_shapes=[
            pltpu.VMEM((TOP, TOKS), jnp.int32),
            pltpu.VMEM((EXP, TOKS), f32),
            pltpu.VMEM((TOKS, FEAT), bf16),
            pltpu.VMEM((EXP, TOKS), f32),
            pltpu.VMEM((EXP, TOKS), f32),
            pltpu.SemaphoreType.DMA((3,)),
        ],
        compiler_params=pltpu.CompilerParams(vmem_limit_bytes=60 * MIB),
        cost_estimate=pl.CostEstimate(flops=500_000_000, bytes_accessed=2_700_000, transcendentals=0),
    )(ids, scores, grad)


def order_kernel(x_ref, y_ref):
    i = lax.broadcasted_iota(jnp.int32, (BLOCK, BLOCK), 0)
    j = lax.broadcasted_iota(jnp.int32, (BLOCK, BLOCK), 1)
    e = i - 8 * MAIN
    origin = jnp.where(i < 8 * MAIN, i // MAIN * MOST + i % MAIN, e // EXTRA * MOST + MAIN + e % EXTRA)
    move = jnp.where(origin == j, 1.0, 0.0).astype(bf16)
    y_ref[...] = jnp.dot(move, x_ref[...], preferred_element_type=f32).astype(bf16)


def order(hidden):
    return pl.pallas_call(
        order_kernel,
        grid=(GROUPS,),
        in_specs=[pl.BlockSpec((BLOCK, HID), lambda i: (i, 0))],
        out_specs=pl.BlockSpec((BLOCK, HID), lambda i: (i, 0)),
        out_shape=jax.ShapeDtypeStruct((SLOTS, HID), bf16),
        cost_estimate=pl.CostEstimate(flops=500_000_000, bytes_accessed=5_300_000, transcendentals=0),
    )(hidden)


def restore_kernel(x_ref, y_ref):
    j = lax.broadcasted_iota(jnp.int32, (BLOCK, BLOCK), 0)
    i = lax.broadcasted_iota(jnp.int32, (BLOCK, BLOCK), 1)
    e = i - 8 * MAIN
    origin = jnp.where(i < 8 * MAIN, i // MAIN * MOST + i % MAIN, e // EXTRA * MOST + MAIN + e % EXTRA)
    move = jnp.where(origin == j, 1.0, 0.0).astype(bf16)
    y_ref[...] = jnp.dot(move, x_ref[...], preferred_element_type=f32).astype(bf16)


def restore(x):
    return pl.pallas_call(
        restore_kernel,
        out_shape=jax.ShapeDtypeStruct((BLOCK, HID), bf16),
        compiler_params=pltpu.CompilerParams(vmem_limit_bytes=4 * MIB),
        cost_estimate=pl.CostEstimate(flops=60_000_000, bytes_accessed=660_000, transcendentals=0),
    )(x)


PARTS = 2
CHUNK = SLOTS // PARTS
PAIR = EXP // PARTS
SLOT_ROWS = 16


def expert_kernel(
    recv_any, hidden_any, down_any, part_any, slot_ref, rows_any,
    recv_ref, hidden_ref, down_ref, part_ref, rows_ref, in_sems, out_sems,
):
    come, saved, stores = [], [], []
    for c in range(PARTS):
        at = slice(c * PAIR, (c + 1) * PAIR)
        come.append(pltpu.make_async_copy(recv_any.at[at], recv_ref.at[at], in_sems.at[0, c]))
        at = slice(c * CHUNK, (c + 1) * CHUNK)
        saved.append(pltpu.make_async_copy(hidden_any.at[at], hidden_ref.at[at], in_sems.at[1, c]))
        stores.append(
            [
                pltpu.make_async_copy(rows_ref.at[at], rows_any.at[at], out_sems.at[0, c]),
                pltpu.make_async_copy(part_ref.at[at], part_any.at[at], out_sems.at[1, c]),
            ]
        )
    weights = pltpu.make_async_copy(down_any, down_ref, in_sems.at[2, 0])
    come[0].start()
    weights.start()
    for c in range(PARTS):
        if c:
            come[c].start()
        saved[c].start()

    i = lax.broadcasted_iota(jnp.int32, (LANES, LANES), 0)
    j = lax.broadcasted_iota(jnp.int32, (LANES, LANES), 1)
    q, source, r = i // 32, i % 32 // EXTRA, i % EXTRA
    move = jnp.where(source * MAIN + q * EXTRA + r == j, 1.0, 0.0).astype(bf16)
    ones = jnp.ones((8, LANES), bf16)
    slot_ref[...] = jnp.zeros_like(slot_ref)
    for c in range(PARTS):
        at = slice(c * CHUNK, (c + 1) * CHUNK)
        come[c].wait()
        for g in range(c * PAIR // 8, (c + 1) * PAIR // 8):
            some = slice(8 * g, 8 * g + 8)
            for j in range(COLS):
                rows_ref[BLOCK * g : BLOCK * g + LANES, LANES * j : LANES * (j + 1)] = recv_ref[
                    some, MAIN * j : MAIN * (j + 1), :
                ].reshape(LANES, LANES)
            for part in range(2):
                start = COLS * MAIN + part * MAIN
                x = recv_ref[some, start : start + MAIN, :].reshape(LANES, LANES)
                y = jnp.dot(move, x, preferred_element_type=f32).astype(bf16)
                for q in range(4):
                    j = part * 4 + q
                    if j < COLS:
                        rows_ref[BLOCK * g + LANES : BLOCK * (g + 1), LANES * j : LANES * (j + 1)] = y[
                            32 * q : 32 * (q + 1)
                        ]
        stores[c][0].start()
        if c == 0:
            weights.wait()
        saved[c].wait()
        part = jnp.dot(rows_ref[at, :], down_ref[...], preferred_element_type=f32)
        both = part * hidden_ref[at, :].astype(f32)
        rest = sum(both[:, LANES * q : LANES * (q + 1)] for q in range(HID // LANES))
        part_ref[at, :] = part.astype(bf16)
        stores[c][1].start()
        sums = jnp.zeros((8, CHUNK), f32)
        for _ in range(3):
            term = rest.astype(bf16)
            rest = rest - term.astype(f32)
            sums = sums + lax.dot_general(ones, term, (((1,), (1,)), ((), ())), preferred_element_type=f32)
        for h in range(CHUNK // BLOCK):
            g = CHUNK // BLOCK * c + h
            slot_ref[:, g, :] = sums[:, BLOCK * h : BLOCK * h + LANES]
            slot_ref[:, GROUPS + g, : BLOCK - LANES] = sums[:, BLOCK * h + LANES : BLOCK * (h + 1)]
    for pair in stores:
        for store in pair:
            store.wait()


EXPERT_LIMIT = 52


def expert(recv, hidden, down_t):
    any_space = pl.BlockSpec(memory_space=pl.ANY)
    return pl.pallas_call(
        expert_kernel,
        in_specs=[any_space] * 3,
        out_specs=[any_space, pl.BlockSpec(memory_space=pltpu.VMEM), any_space],
        out_shape=[
            jax.ShapeDtypeStruct((SLOTS, HID), bf16),
            jax.ShapeDtypeStruct((GROUPS, SLOT_ROWS, LANES), f32),
            jax.ShapeDtypeStruct((SLOTS, FEAT), bf16),
        ],
        scratch_shapes=[
            pltpu.VMEM((EXP, PIECE, LANES), bf16),
            pltpu.VMEM((SLOTS, HID), bf16),
            pltpu.VMEM((FEAT, HID), bf16),
            pltpu.VMEM((SLOTS, HID), bf16),
            pltpu.VMEM((SLOTS, FEAT), bf16),
            pltpu.SemaphoreType.DMA((3, PARTS)),
            pltpu.SemaphoreType.DMA((2, PARTS)),
        ],
        compiler_params=pltpu.CompilerParams(vmem_limit_bytes=EXPERT_LIMIT * MIB),
        cost_estimate=pl.CostEstimate(flops=2_400_000_000, bytes_accessed=11_000_000, transcendentals=0),
    )(recv, hidden, down_t)


def spread_kernel(slot_ref, out_ref):
    summed = jnp.sum(slot_ref[...], axis=0)
    main = summed[:GROUPS]
    extra = pltpu.roll(summed[GROUPS:], MAIN, 1)
    lane = lax.broadcasted_iota(jnp.int32, (GROUPS, LANES), 1)
    for place in range(8):
        a = pltpu.roll(main, -MAIN * place % LANES, 1) if place else main
        b = pltpu.roll(extra, -EXTRA * place % LANES, 1) if place else extra
        value = jnp.where(lane < MAIN, a, b)
        for g in range(GROUPS):
            out_ref[8 * g + place : 8 * g + place + 1, :] = value[g : g + 1]


def spread(slot):
    return pl.pallas_call(
        spread_kernel,
        out_shape=jax.ShapeDtypeStruct((EXP, LANES), f32),
        compiler_params=pltpu.CompilerParams(vmem_limit_bytes=2 * MIB),
        cost_estimate=pl.CostEstimate(flops=10_000, bytes_accessed=100_000, transcendentals=0),
    )(slot)


def gate_kernel(ids_ref, scores_ref, back_ref, tokens_ref, out_ref):
    hit, chosen, total, weights, rank = routing(ids_ref[...], scores_ref[...])
    route = jnp.zeros((EXP, TOKS), f32)
    for r in range(MOST):
        route = route + jnp.where(rank == float(r), back_ref[:, r : r + 1], 0.0)
    route = jnp.where(hit, route / jnp.where(hit, weights, 1.0), 0.0)
    mixed = jnp.sum(route * chosen, axis=0, keepdims=True) / total
    score = route_scale / total * (route - mixed)
    logit = (score * chosen * (1.0 - chosen)).astype(bf16)
    out_ref[...] = jnp.dot(logit, tokens_ref[...], preferred_element_type=f32)


def gate(ids, scores, back, tokens):
    return pl.pallas_call(
        gate_kernel,
        out_shape=jax.ShapeDtypeStruct((EXP, FEAT), f32),
        compiler_params=pltpu.CompilerParams(vmem_limit_bytes=4 * MIB),
        cost_estimate=pl.CostEstimate(flops=15_000_000, bytes_accessed=560_000, transcendentals=0),
    )(ids, scores, back, tokens)


def body(grad_out, tokens, scores, expert_ids, hidden_act, down_weight):
    both = ("ep", "node")
    exchange = functools.partial(lax.all_to_all, split_axis=0, concat_axis=0, tiled=True)
    ids, scores = expert_ids.T, scores.T
    recv = exchange(pack(ids, scores, grad_out), both)
    hidden = order(hidden_act[0])
    part, slot, rows = expert(recv, hidden, down_weight[0].T)
    slot = exchange(slot, "dp")
    summed = lax.psum_scatter(part, "dp", scatter_dimension=0, tiled=True)
    back = exchange(spread(slot), both)
    weight_grad = lax.dot_general(hidden, rows, (((0,), (0,)), ((), ())), preferred_element_type=f32)
    weight_grad = weight_grad.astype(bf16)[None]
    back, weight_grad = lax.optimization_barrier((back, weight_grad))
    gate_rows = exchange(gate(ids, scores, back, tokens), both)
    gate_row = jnp.sum(gate_rows, axis=0, keepdims=True)
    gate_row, summed = lax.optimization_barrier((gate_row, summed))
    gate_grad = exchange(jnp.broadcast_to(gate_row, (EXP, FEAT)), both)
    hidden_grad = restore(summed)[None]
    return (weight_grad, hidden_grad, gate_grad)


def solution(mesh):
    return jax.shard_map(
        body,
        mesh=mesh,
        in_specs=(
            P(("ep", "node"), "dp"),
            P(("ep", "node"), "dp"),
            P(("ep", "node"), None),
            P(("ep", "node"), None),
            P(("ep", "node"), None, None),
            P(("ep", "node"), None, "dp"),
        ),
        out_specs=(P(("ep", "node"), None, "dp"), P(("ep", "node"), "dp", None), P(None, "dp")),
        check_vma=False,
    )
```

```python
import functools

import jax
import jax.numpy as jnp
from jax import lax
from jax.experimental import pallas as pl
from jax.experimental.pallas import tpu as pltpu
from jax.sharding import PartitionSpec as P

route_scale = 2.5
TOKS = 128
TOP = 8
EXP = 64
MOST = 20
MAIN = 16
EXTRA = MOST - MAIN
FEAT = 896
LANES = 128
COLS = FEAT // LANES
PIECE = COLS * MAIN + 32
HID = 1024
SLOTS = EXP * MOST
GROUPS = 8
BLOCK = SLOTS // GROUPS
ROW = 4
MIB = 1024 * 1024
bf16, f32 = jnp.bfloat16, jnp.float32


def routing(ids, scores):
    expert = lax.broadcasted_iota(jnp.int32, (EXP, TOKS), 0)
    hit = ids[0:1, :] == expert
    for k in range(1, TOP):
        hit = hit | (ids[k : k + 1, :] == expert)
    earlier = (
        lax.broadcasted_iota(jnp.int32, (TOKS, TOKS), 0) < lax.broadcasted_iota(jnp.int32, (TOKS, TOKS), 1)
    )
    ones = jnp.where(hit, 1.0, 0.0)
    rank = jnp.dot(
        ones.astype(bf16), jnp.where(earlier, 1.0, 0.0).astype(bf16), preferred_element_type=f32
    )
    rank = jnp.where(hit, rank, -1.0)
    chosen = jnp.where(hit, scores, 0.0)
    total = jnp.sum(chosen, axis=0, keepdims=True)
    weights = (route_scale * chosen / total).astype(bf16).astype(f32)
    return hit, chosen, total, weights, rank


def pack_kernel(
    ids_any, scores_any, grad_any, send_any, ids_ref, scores_ref, grad_ref, rank_ref, weight_ref, send_ref, sems, out_sems
):
    copies = [
        pltpu.make_async_copy(ids_any, ids_ref, sems.at[0]),
        pltpu.make_async_copy(scores_any, scores_ref, sems.at[1]),
        pltpu.make_async_copy(grad_any, grad_ref, sems.at[2]),
    ]
    for copy in copies:
        copy.start()
    copies[0].wait()
    copies[1].wait()
    _, _, _, weights, rank = routing(ids_ref[...], scores_ref[...])
    rank_ref[...] = rank
    weight_ref[...] = weights
    copies[2].wait()
    grad = grad_ref[...]
    row = lax.broadcasted_iota(jnp.int32, (8, MAIN, TOKS), 1)
    main_rank = row.astype(f32)
    extra_rank = (MAIN + row % EXTRA).astype(f32)
    quarter = lax.broadcasted_iota(jnp.int32, (8 * MAIN, LANES), 0) % MAIN // EXTRA

    outs = []
    for i in range(EXP // 8):
        at = slice(8 * i, 8 * i + 8)
        ranks = rank_ref[at, :][:, None, :]
        gains = weight_ref[at, :][:, None, :]
        place = jnp.where(ranks == main_rank, gains, 0.0).reshape(8 * MAIN, TOKS).astype(bf16)
        rows = jnp.dot(place, grad, preferred_element_type=f32)
        for j in range(COLS):
            send_ref[at, MAIN * j : MAIN * (j + 1), :] = (
                rows[:, LANES * j : LANES * (j + 1)].astype(bf16).reshape(8, MAIN, LANES)
            )
        place = jnp.where(ranks == extra_rank, gains, 0.0).reshape(8 * MAIN, TOKS).astype(bf16)
        rows = jnp.dot(place, grad, preferred_element_type=f32)
        for part in range(2):
            mixed = jnp.zeros((8 * MAIN, LANES), f32)
            for q in range(4):
                j = part * 4 + q
                if j < COLS:
                    mixed = jnp.where(quarter == q, rows[:, LANES * j : LANES * (j + 1)], mixed)
            start = COLS * MAIN + part * MAIN
            send_ref[at, start : start + MAIN, :] = mixed.astype(bf16).reshape(8, MAIN, LANES)
        outs.append(pltpu.make_async_copy(send_ref.at[at], send_any.at[at], out_sems.at[i]))
        outs[i].start()
    for out in outs:
        out.wait()


def pack(ids, scores, grad):
    return pl.pallas_call(
        pack_kernel,
        in_specs=[pl.BlockSpec(memory_space=pl.ANY)] * 3,
        out_specs=pl.BlockSpec(memory_space=pl.ANY),
        out_shape=jax.ShapeDtypeStruct((EXP, PIECE, LANES), bf16),
        scratch_shapes=[
            pltpu.VMEM((TOP, TOKS), jnp.int32),
            pltpu.VMEM((EXP, TOKS), f32),
            pltpu.VMEM((TOKS, FEAT), bf16),
            pltpu.VMEM((EXP, TOKS), f32),
            pltpu.VMEM((EXP, TOKS), f32),
            pltpu.VMEM((EXP, PIECE, LANES), bf16),
            pltpu.SemaphoreType.DMA((3,)),
            pltpu.SemaphoreType.DMA((EXP // 8,)),
        ],
        compiler_params=pltpu.CompilerParams(vmem_limit_bytes=60 * MIB),
        cost_estimate=pl.CostEstimate(flops=500_000_000, bytes_accessed=2_700_000, transcendentals=0),
    )(ids, scores, grad)


def order_kernel(x_ref, y_ref):
    i = lax.broadcasted_iota(jnp.int32, (BLOCK, BLOCK), 0)
    j = lax.broadcasted_iota(jnp.int32, (BLOCK, BLOCK), 1)
    e = i - 8 * MAIN
    origin = jnp.where(i < 8 * MAIN, i // MAIN * MOST + i % MAIN, e // EXTRA * MOST + MAIN + e % EXTRA)
    move = jnp.where(origin == j, 1.0, 0.0).astype(bf16)
    y_ref[...] = jnp.dot(move, x_ref[...], preferred_element_type=f32).astype(bf16)


def order(hidden):
    return pl.pallas_call(
        order_kernel,
        grid=(GROUPS,),
        in_specs=[pl.BlockSpec((BLOCK, HID), lambda i: (i, 0))],
        out_specs=pl.BlockSpec((BLOCK, HID), lambda i: (i, 0)),
        out_shape=jax.ShapeDtypeStruct((SLOTS, HID), bf16),
        cost_estimate=pl.CostEstimate(flops=500_000_000, bytes_accessed=5_300_000, transcendentals=0),
    )(hidden)


def restore_kernel(x_ref, y_ref):
    j = lax.broadcasted_iota(jnp.int32, (BLOCK, BLOCK), 0)
    i = lax.broadcasted_iota(jnp.int32, (BLOCK, BLOCK), 1)
    e = i - 8 * MAIN
    origin = jnp.where(i < 8 * MAIN, i // MAIN * MOST + i % MAIN, e // EXTRA * MOST + MAIN + e % EXTRA)
    move = jnp.where(origin == j, 1.0, 0.0).astype(bf16)
    y_ref[...] = jnp.dot(move, x_ref[...], preferred_element_type=f32).astype(bf16)


def restore(x):
    return pl.pallas_call(
        restore_kernel,
        out_shape=jax.ShapeDtypeStruct((BLOCK, HID), bf16),
        compiler_params=pltpu.CompilerParams(vmem_limit_bytes=4 * MIB),
        cost_estimate=pl.CostEstimate(flops=60_000_000, bytes_accessed=660_000, transcendentals=0),
    )(x)


PARTS = 2
CHUNK = SLOTS // PARTS
PAIR = EXP // PARTS
SLOT_ROWS = 16


def expert_kernel(
    recv_any, hidden_any, down_any, part_any, slot_ref, rows_any,
    recv_ref, hidden_ref, down_ref, part_ref, rows_ref, in_sems, out_sems,
):
    come, saved, stores = [], [], []
    for c in range(PARTS):
        at = slice(c * PAIR, (c + 1) * PAIR)
        come.append(pltpu.make_async_copy(recv_any.at[at], recv_ref.at[at], in_sems.at[0, c]))
        at = slice(c * CHUNK, (c + 1) * CHUNK)
        saved.append(pltpu.make_async_copy(hidden_any.at[at], hidden_ref.at[at], in_sems.at[1, c]))
        stores.append(
            [
                pltpu.make_async_copy(rows_ref.at[at], rows_any.at[at], out_sems.at[0, c]),
                pltpu.make_async_copy(part_ref.at[at], part_any.at[at], out_sems.at[1, c]),
            ]
        )
    weights = pltpu.make_async_copy(down_any, down_ref, in_sems.at[2, 0])
    come[0].start()
    weights.start()
    for c in range(PARTS):
        if c:
            come[c].start()
        saved[c].start()

    i = lax.broadcasted_iota(jnp.int32, (LANES, LANES), 0)
    j = lax.broadcasted_iota(jnp.int32, (LANES, LANES), 1)
    q, source, r = i // 32, i % 32 // EXTRA, i % EXTRA
    move = jnp.where(source * MAIN + q * EXTRA + r == j, 1.0, 0.0).astype(bf16)
    ones = jnp.ones((8, LANES), bf16)
    slot_ref[...] = jnp.zeros_like(slot_ref)
    for c in range(PARTS):
        at = slice(c * CHUNK, (c + 1) * CHUNK)
        come[c].wait()
        for g in range(c * PAIR // 8, (c + 1) * PAIR // 8):
            some = slice(8 * g, 8 * g + 8)
            for j in range(COLS):
                rows_ref[BLOCK * g : BLOCK * g + LANES, LANES * j : LANES * (j + 1)] = recv_ref[
                    some, MAIN * j : MAIN * (j + 1), :
                ].reshape(LANES, LANES)
            for part in range(2):
                start = COLS * MAIN + part * MAIN
                x = recv_ref[some, start : start + MAIN, :].reshape(LANES, LANES)
                y = jnp.dot(move, x, preferred_element_type=f32).astype(bf16)
                for q in range(4):
                    j = part * 4 + q
                    if j < COLS:
                        rows_ref[BLOCK * g + LANES : BLOCK * (g + 1), LANES * j : LANES * (j + 1)] = y[
                            32 * q : 32 * (q + 1)
                        ]
        stores[c][0].start()
        if c == 0:
            weights.wait()
        saved[c].wait()
        part = jnp.dot(rows_ref[at, :], down_ref[...], preferred_element_type=f32)
        both = part * hidden_ref[at, :].astype(f32)
        rest = sum(both[:, LANES * q : LANES * (q + 1)] for q in range(HID // LANES))
        part_ref[at, :] = part.astype(bf16)
        stores[c][1].start()
        sums = jnp.zeros((8, CHUNK), f32)
        for _ in range(3):
            term = rest.astype(bf16)
            rest = rest - term.astype(f32)
            sums = sums + lax.dot_general(ones, term, (((1,), (1,)), ((), ())), preferred_element_type=f32)
        for h in range(CHUNK // BLOCK):
            g = CHUNK // BLOCK * c + h
            slot_ref[:, g, :] = sums[:, BLOCK * h : BLOCK * h + LANES]
            slot_ref[:, GROUPS + g, : BLOCK - LANES] = sums[:, BLOCK * h + LANES : BLOCK * (h + 1)]
    for pair in stores:
        for store in pair:
            store.wait()


EXPERT_LIMIT = 52


def expert(recv, hidden, down_t):
    any_space = pl.BlockSpec(memory_space=pl.ANY)
    return pl.pallas_call(
        expert_kernel,
        in_specs=[any_space] * 3,
        out_specs=[any_space, pl.BlockSpec(memory_space=pltpu.VMEM), any_space],
        out_shape=[
            jax.ShapeDtypeStruct((SLOTS, HID), bf16),
            jax.ShapeDtypeStruct((GROUPS, SLOT_ROWS, LANES), f32),
            jax.ShapeDtypeStruct((SLOTS, FEAT), bf16),
        ],
        scratch_shapes=[
            pltpu.VMEM((EXP, PIECE, LANES), bf16),
            pltpu.VMEM((SLOTS, HID), bf16),
            pltpu.VMEM((FEAT, HID), bf16),
            pltpu.VMEM((SLOTS, HID), bf16),
            pltpu.VMEM((SLOTS, FEAT), bf16),
            pltpu.SemaphoreType.DMA((3, PARTS)),
            pltpu.SemaphoreType.DMA((2, PARTS)),
        ],
        compiler_params=pltpu.CompilerParams(vmem_limit_bytes=EXPERT_LIMIT * MIB),
        cost_estimate=pl.CostEstimate(flops=2_400_000_000, bytes_accessed=11_000_000, transcendentals=0),
    )(recv, hidden, down_t)


def spread_kernel(slot_ref, out_ref):
    summed = jnp.sum(slot_ref[...], axis=0)
    main = summed[:GROUPS]
    extra = pltpu.roll(summed[GROUPS:], MAIN, 1)
    lane = lax.broadcasted_iota(jnp.int32, (GROUPS, LANES), 1)
    span = lane[:1] // 32
    for place in range(8):
        a = pltpu.roll(main, -MAIN * place % LANES, 1) if place else main
        b = pltpu.roll(extra, -EXTRA * place % LANES, 1) if place else extra
        value = jnp.where(lane < MAIN, a, b)
        moved = [pltpu.roll(value, 32 * k, 1) if k else value for k in range(ROW)]
        for x in range(ROW):
            for high in range(2):
                line = jnp.zeros((1, LANES), f32)
                for k in range(ROW):
                    g = (x - k) % ROW * 2 + high
                    line = jnp.where(span == k, moved[k][g : g + 1], line)
                at = EXP // ROW * x + 8 * high + place
                out_ref[at : at + 1, :] = line


def spread(slot):
    return pl.pallas_call(
        spread_kernel,
        out_shape=jax.ShapeDtypeStruct((EXP, LANES), f32),
        compiler_params=pltpu.CompilerParams(vmem_limit_bytes=2 * MIB),
        cost_estimate=pl.CostEstimate(flops=10_000, bytes_accessed=100_000, transcendentals=0),
    )(slot)


def gate_kernel(x_ref, table_ref, tables_ref, back_ref, tokens_ref, others_ref, out_ref, logit_ref):
    for k in range(ROW):
        table = tables_ref[k - 1] if k else table_ref[...]
        hit, chosen, total, weights, rank = routing(table[EXP:].astype(jnp.int32), table[:EXP])
        route = jnp.zeros((EXP, TOKS), f32)
        for r in range(MOST):
            at = 32 * k + r
            route = route + jnp.where(rank == float(r), back_ref[:, at : at + 1], 0.0)
        route = jnp.where(hit, route / jnp.where(hit, weights, 1.0), 0.0)
        mixed = jnp.sum(route * chosen, axis=0, keepdims=True) / total
        score = route_scale / total * (route - mixed)
        logit_ref[:, TOKS * k : TOKS * (k + 1)] = (score * chosen * (1.0 - chosen)).astype(bf16)
    own = pl.ds(pl.multiple_of(x_ref[0] * (EXP // ROW), EXP // ROW), EXP // ROW)
    grad = jnp.zeros((EXP // ROW, FEAT), f32)
    for k in range(ROW):
        tokens = others_ref[k - 1] if k else tokens_ref[...]
        grad = grad + jnp.dot(logit_ref[own, TOKS * k : TOKS * (k + 1)], tokens, preferred_element_type=f32)
    out_ref[...] = grad


def gate(x, table, tables, back, tokens, others):
    return pl.pallas_call(
        gate_kernel,
        in_specs=[pl.BlockSpec(memory_space=pltpu.SMEM)] + [pl.BlockSpec(memory_space=pltpu.VMEM)] * 5,
        out_shape=jax.ShapeDtypeStruct((EXP // ROW, FEAT), f32),
        scratch_shapes=[pltpu.VMEM((EXP, ROW * TOKS), bf16)],
        compiler_params=pltpu.CompilerParams(vmem_limit_bytes=6 * MIB),
        cost_estimate=pl.CostEstimate(flops=30_000_000, bytes_accessed=1_200_000, transcendentals=0),
    )(x, table, tables, back, tokens, others)


def body(grad_out, tokens, scores, expert_ids, hidden_act, down_weight):
    both = ("x", "y", "node")
    exchange = functools.partial(lax.all_to_all, split_axis=0, concat_axis=0, tiled=True)

    def gather(v):
        return jnp.stack([lax.ppermute(v, "x", [(i, (i + k) % ROW) for i in range(ROW)]) for k in range(1, ROW)])

    ids, scores = expert_ids.T, scores.T
    recv = exchange(pack(ids, scores, grad_out), both)
    hidden = order(hidden_act[0])
    table = jnp.concatenate([scores, ids.astype(f32)], axis=0)
    hidden, far_tokens, far_table = lax.optimization_barrier((hidden, tokens, table))
    others, tables = gather(far_tokens), gather(far_table)
    recv, others, tables = lax.optimization_barrier((recv, others, tables))
    part, slot, rows = expert(recv, hidden, down_weight[0].T)
    slot = exchange(slot, "dp")
    summed = lax.psum_scatter(part, "dp", scatter_dimension=0, tiled=True)
    back = exchange(spread(slot), both)
    weight_grad = lax.dot_general(hidden, rows, (((0,), (0,)), ((), ())), preferred_element_type=f32)
    weight_grad = weight_grad.astype(bf16)[None]
    back, weight_grad = lax.optimization_barrier((back, weight_grad))
    x = lax.axis_index("x").astype(jnp.int32).reshape(1)
    gate_rows = exchange(gate(x, table, tables, back, tokens, others), ("y", "node"))
    gate_row = jnp.sum(gate_rows, axis=0, keepdims=True)
    gate_row, summed = lax.optimization_barrier((gate_row, summed))
    gate_grad = exchange(jnp.broadcast_to(gate_row, (EXP, FEAT)), both)
    hidden_grad = restore(summed)[None]
    return (weight_grad, hidden_grad, gate_grad)


def solution(mesh):
    devices = mesh.devices.reshape(ROW, -1, *mesh.devices.shape[1:])
    both = ("x", "y", "node")
    return jax.shard_map(
        body,
        mesh=jax.sharding.Mesh(devices, (*both, "dp")),
        in_specs=(P(both, "dp"), P(both, "dp"), P(both, None), P(both, None), P(both, None, None), P(both, None, "dp")),
        out_specs=(P(both, None, "dp"), P(both, "dp", None), P(None, "dp")),
        check_vma=False,
    )
```

```python
import functools

import jax
import jax.numpy as jnp
from jax import lax
from jax.experimental import pallas as pl
from jax.experimental.pallas import tpu as pltpu
from jax.sharding import PartitionSpec as P

route_scale = 2.5
TOKS = 128
TOP = 8
EXP = 64
MOST = 20
MAIN = 16
EXTRA = MOST - MAIN
FEAT = 896
LANES = 128
COLS = FEAT // LANES
PIECE = COLS * MAIN + 32
HID = 1024
SLOTS = EXP * MOST
GROUPS = 8
BLOCK = SLOTS // GROUPS
ROW = 4
MIB = 1024 * 1024
bf16, f32 = jnp.bfloat16, jnp.float32


def routing(ids, scores):
    expert = lax.broadcasted_iota(jnp.int32, (EXP, TOKS), 0)
    hit = ids[0:1, :] == expert
    for k in range(1, TOP):
        hit = hit | (ids[k : k + 1, :] == expert)
    earlier = (
        lax.broadcasted_iota(jnp.int32, (TOKS, TOKS), 0) < lax.broadcasted_iota(jnp.int32, (TOKS, TOKS), 1)
    )
    ones = jnp.where(hit, 1.0, 0.0)
    rank = jnp.dot(
        ones.astype(bf16), jnp.where(earlier, 1.0, 0.0).astype(bf16), preferred_element_type=f32
    )
    rank = jnp.where(hit, rank, -1.0)
    chosen = jnp.where(hit, scores, 0.0)
    total = jnp.sum(chosen, axis=0, keepdims=True)
    weights = (route_scale * chosen / total).astype(bf16).astype(f32)
    return hit, chosen, total, weights, rank


def pack_kernel(
    ids_any, scores_any, grad_any, send_any, ids_ref, scores_ref, grad_ref, rank_ref, weight_ref, send_ref, sems, out_sems
):
    copies = [
        pltpu.make_async_copy(ids_any, ids_ref, sems.at[0]),
        pltpu.make_async_copy(scores_any, scores_ref, sems.at[1]),
        pltpu.make_async_copy(grad_any, grad_ref, sems.at[2]),
    ]
    for copy in copies:
        copy.start()
    copies[0].wait()
    copies[1].wait()
    _, _, _, weights, rank = routing(ids_ref[...], scores_ref[...])
    rank_ref[...] = rank
    weight_ref[...] = weights
    copies[2].wait()
    grad = grad_ref[...]
    row = lax.broadcasted_iota(jnp.int32, (8, MAIN, TOKS), 1)
    main_rank = row.astype(f32)
    extra_rank = (MAIN + row % EXTRA).astype(f32)
    quarter = lax.broadcasted_iota(jnp.int32, (8 * MAIN, LANES), 0) % MAIN // EXTRA

    outs = []
    for i in range(EXP // 8):
        at = slice(8 * i, 8 * i + 8)
        ranks = rank_ref[at, :][:, None, :]
        gains = weight_ref[at, :][:, None, :]
        place = jnp.where(ranks == main_rank, gains, 0.0).reshape(8 * MAIN, TOKS).astype(bf16)
        rows = jnp.dot(place, grad, preferred_element_type=f32)
        for j in range(COLS):
            send_ref[at, MAIN * j : MAIN * (j + 1), :] = (
                rows[:, LANES * j : LANES * (j + 1)].astype(bf16).reshape(8, MAIN, LANES)
            )
        place = jnp.where(ranks == extra_rank, gains, 0.0).reshape(8 * MAIN, TOKS).astype(bf16)
        rows = jnp.dot(place, grad, preferred_element_type=f32)
        for part in range(2):
            mixed = jnp.zeros((8 * MAIN, LANES), f32)
            for q in range(4):
                j = part * 4 + q
                if j < COLS:
                    mixed = jnp.where(quarter == q, rows[:, LANES * j : LANES * (j + 1)], mixed)
            start = COLS * MAIN + part * MAIN
            send_ref[at, start : start + MAIN, :] = mixed.astype(bf16).reshape(8, MAIN, LANES)
        outs.append(pltpu.make_async_copy(send_ref.at[at], send_any.at[at], out_sems.at[i]))
        outs[i].start()
    for out in outs:
        out.wait()


def pack(ids, scores, grad):
    return pl.pallas_call(
        pack_kernel,
        in_specs=[pl.BlockSpec(memory_space=pl.ANY)] * 3,
        out_specs=pl.BlockSpec(memory_space=pl.ANY),
        out_shape=jax.ShapeDtypeStruct((EXP, PIECE, LANES), bf16),
        scratch_shapes=[
            pltpu.VMEM((TOP, TOKS), jnp.int32),
            pltpu.VMEM((EXP, TOKS), f32),
            pltpu.VMEM((TOKS, FEAT), bf16),
            pltpu.VMEM((EXP, TOKS), f32),
            pltpu.VMEM((EXP, TOKS), f32),
            pltpu.VMEM((EXP, PIECE, LANES), bf16),
            pltpu.SemaphoreType.DMA((3,)),
            pltpu.SemaphoreType.DMA((EXP // 8,)),
        ],
        compiler_params=pltpu.CompilerParams(vmem_limit_bytes=60 * MIB),
        cost_estimate=pl.CostEstimate(flops=500_000_000, bytes_accessed=2_700_000, transcendentals=0),
    )(ids, scores, grad)


def source_order(i):
    e = i - 8 * MAIN
    return jnp.where(i < 8 * MAIN, i // MAIN * MOST + i % MAIN, e // EXTRA * MOST + MAIN + e % EXTRA)


def order_kernel(x_ref, y_ref):
    i = lax.broadcasted_iota(jnp.int32, (BLOCK, BLOCK), 0)
    j = lax.broadcasted_iota(jnp.int32, (BLOCK, BLOCK), 1)
    move = jnp.where(source_order(i) == j, 1.0, 0.0).astype(bf16)
    y_ref[...] = jnp.dot(move, x_ref[...], preferred_element_type=f32).astype(bf16)


def order(hidden):
    return pl.pallas_call(
        order_kernel,
        grid=(GROUPS,),
        in_specs=[pl.BlockSpec((BLOCK, HID), lambda i: (i, 0))],
        out_specs=pl.BlockSpec((BLOCK, HID), lambda i: (i, 0)),
        out_shape=jax.ShapeDtypeStruct((SLOTS, HID), bf16),
        cost_estimate=pl.CostEstimate(flops=500_000_000, bytes_accessed=5_300_000, transcendentals=0),
    )(hidden)


PARTS = 2
CHUNK = SLOTS // PARTS
PAIR = EXP // PARTS
SLOT_ROWS = 16


def expert_kernel(
    recv_any, hidden_any, down_ref, part_any, slot_ref, rows_any,
    recv_ref, hidden_ref, part_ref, rows_ref, in_sems, out_sems,
):
    come, saved, stores = [], [], []
    for c in range(PARTS):
        at = slice(c * PAIR, (c + 1) * PAIR)
        come.append(pltpu.make_async_copy(recv_any.at[at], recv_ref.at[at], in_sems.at[0, c]))
        at = slice(c * CHUNK, (c + 1) * CHUNK)
        saved.append(pltpu.make_async_copy(hidden_any.at[at], hidden_ref.at[at], in_sems.at[1, c]))
        stores.append(
            [
                pltpu.make_async_copy(rows_ref.at[at], rows_any.at[at], out_sems.at[0, c]),
                pltpu.make_async_copy(part_ref.at[at], part_any.at[at], out_sems.at[1, c]),
            ]
        )
    for c in range(PARTS):
        come[c].start()
        saved[c].start()

    i = lax.broadcasted_iota(jnp.int32, (LANES, LANES), 0)
    j = lax.broadcasted_iota(jnp.int32, (LANES, LANES), 1)
    q, source, r = i // 32, i % 32 // EXTRA, i % EXTRA
    move = jnp.where(source * MAIN + q * EXTRA + r == j, 1.0, 0.0).astype(bf16)
    j = lax.broadcasted_iota(jnp.int32, (BLOCK, BLOCK), 0)
    back = jnp.where(source_order(lax.broadcasted_iota(jnp.int32, (BLOCK, BLOCK), 1)) == j, 1.0, 0.0).astype(bf16)
    ones = jnp.ones((8, LANES), bf16)
    slot_ref[...] = jnp.zeros_like(slot_ref)
    for c in range(PARTS):
        come[c].wait()
        for g in range(c * PAIR // 8, (c + 1) * PAIR // 8):
            some = slice(8 * g, 8 * g + 8)
            for j in range(COLS):
                rows_ref[BLOCK * g : BLOCK * g + LANES, LANES * j : LANES * (j + 1)] = recv_ref[
                    some, MAIN * j : MAIN * (j + 1), :
                ].reshape(LANES, LANES)
            for part in range(2):
                start = COLS * MAIN + part * MAIN
                x = recv_ref[some, start : start + MAIN, :].reshape(LANES, LANES)
                y = jnp.dot(move, x, preferred_element_type=f32).astype(bf16)
                for q in range(4):
                    j = part * 4 + q
                    if j < COLS:
                        rows_ref[BLOCK * g + LANES : BLOCK * (g + 1), LANES * j : LANES * (j + 1)] = y[
                            32 * q : 32 * (q + 1)
                        ]
        stores[c][0].start()
        saved[c].wait()
        terms = []
        for g in range(CHUNK // BLOCK * c, CHUNK // BLOCK * (c + 1)):
            line = slice(BLOCK * g, BLOCK * (g + 1))
            part = jnp.dot(rows_ref[line, :], down_ref[...], preferred_element_type=f32)
            both = part * hidden_ref[line, :].astype(f32)
            terms.append(sum(both[:, LANES * q : LANES * (q + 1)] for q in range(HID // LANES)))
            part_ref[line, :] = jnp.dot(back, part.astype(bf16), preferred_element_type=f32).astype(bf16)
        rest = jnp.concatenate(terms, axis=0)
        stores[c][1].start()
        sums = jnp.zeros((8, CHUNK), f32)
        for _ in range(3):
            term = rest.astype(bf16)
            rest = rest - term.astype(f32)
            sums = sums + lax.dot_general(ones, term, (((1,), (1,)), ((), ())), preferred_element_type=f32)
        for h in range(CHUNK // BLOCK):
            g = CHUNK // BLOCK * c + h
            slot_ref[:, g, :] = sums[:, BLOCK * h : BLOCK * h + LANES]
            slot_ref[:, GROUPS + g, : BLOCK - LANES] = sums[:, BLOCK * h + LANES : BLOCK * (h + 1)]
    for pair in stores:
        for store in pair:
            store.wait()


EXPERT_LIMIT = 52


def expert(recv, hidden, down_t):
    any_space = pl.BlockSpec(memory_space=pl.ANY)
    return pl.pallas_call(
        expert_kernel,
        in_specs=[any_space, any_space, pl.BlockSpec(memory_space=pltpu.VMEM)],
        out_specs=[any_space, pl.BlockSpec(memory_space=pltpu.VMEM), any_space],
        out_shape=[
            jax.ShapeDtypeStruct((SLOTS, HID), bf16),
            jax.ShapeDtypeStruct((GROUPS, SLOT_ROWS, LANES), f32),
            jax.ShapeDtypeStruct((SLOTS, FEAT), bf16),
        ],
        scratch_shapes=[
            pltpu.VMEM((EXP, PIECE, LANES), bf16),
            pltpu.VMEM((SLOTS, HID), bf16),
            pltpu.VMEM((SLOTS, HID), bf16),
            pltpu.VMEM((SLOTS, FEAT), bf16),
            pltpu.SemaphoreType.DMA((2, PARTS)),
            pltpu.SemaphoreType.DMA((2, PARTS)),
        ],
        compiler_params=pltpu.CompilerParams(vmem_limit_bytes=EXPERT_LIMIT * MIB),
        cost_estimate=pl.CostEstimate(flops=2_400_000_000, bytes_accessed=11_000_000, transcendentals=0),
    )(recv, hidden, down_t)


def spread_kernel(slot_ref, out_ref):
    summed = jnp.sum(slot_ref[...], axis=0)
    main = summed[:GROUPS]
    extra = pltpu.roll(summed[GROUPS:], MAIN, 1)
    lane = lax.broadcasted_iota(jnp.int32, (GROUPS, LANES), 1)
    span = lane[:1] // 32
    for place in range(8):
        a = pltpu.roll(main, -MAIN * place % LANES, 1) if place else main
        b = pltpu.roll(extra, -EXTRA * place % LANES, 1) if place else extra
        value = jnp.where(lane < MAIN, a, b)
        moved = [pltpu.roll(value, 32 * k, 1) if k else value for k in range(ROW)]
        for x in range(ROW):
            for high in range(2):
                line = jnp.zeros((1, LANES), f32)
                for k in range(ROW):
                    g = (x - k) % ROW * 2 + high
                    line = jnp.where(span == k, moved[k][g : g + 1], line)
                at = EXP // ROW * x + 8 * high + place
                out_ref[at : at + 1, :] = line


def spread(slot):
    return pl.pallas_call(
        spread_kernel,
        out_shape=jax.ShapeDtypeStruct((EXP, LANES), f32),
        compiler_params=pltpu.CompilerParams(vmem_limit_bytes=2 * MIB),
        cost_estimate=pl.CostEstimate(flops=10_000, bytes_accessed=100_000, transcendentals=0),
    )(slot)


def gate_kernel(x_ref, table_ref, tables_ref, back_ref, tokens_ref, others_ref, out_ref, logit_ref):
    for k in range(ROW):
        table = tables_ref[k - 1] if k else table_ref[...]
        hit, chosen, total, weights, rank = routing(table[EXP:].astype(jnp.int32), table[:EXP])
        route = jnp.zeros((EXP, TOKS), f32)
        for r in range(MOST):
            at = 32 * k + r
            route = route + jnp.where(rank == float(r), back_ref[:, at : at + 1], 0.0)
        route = jnp.where(hit, route / jnp.where(hit, weights, 1.0), 0.0)
        mixed = jnp.sum(route * chosen, axis=0, keepdims=True) / total
        score = route_scale / total * (route - mixed)
        logit_ref[:, TOKS * k : TOKS * (k + 1)] = (score * chosen * (1.0 - chosen)).astype(bf16)
    own = pl.ds(pl.multiple_of(x_ref[0] * (EXP // ROW), EXP // ROW), EXP // ROW)
    grad = jnp.zeros((EXP // ROW, FEAT), f32)
    for k in range(ROW):
        tokens = others_ref[k - 1] if k else tokens_ref[...]
        grad = grad + jnp.dot(logit_ref[own, TOKS * k : TOKS * (k + 1)], tokens, preferred_element_type=f32)
    out_ref[...] = grad


def gate(x, table, tables, back, tokens, others):
    return pl.pallas_call(
        gate_kernel,
        in_specs=[pl.BlockSpec(memory_space=pltpu.SMEM)] + [pl.BlockSpec(memory_space=pltpu.VMEM)] * 5,
        out_shape=jax.ShapeDtypeStruct((EXP // ROW, FEAT), f32),
        scratch_shapes=[pltpu.VMEM((EXP, ROW * TOKS), bf16)],
        compiler_params=pltpu.CompilerParams(vmem_limit_bytes=6 * MIB),
        cost_estimate=pl.CostEstimate(flops=30_000_000, bytes_accessed=1_200_000, transcendentals=0),
    )(x, table, tables, back, tokens, others)


def body(grad_out, tokens, scores, expert_ids, hidden_act, down_weight):
    both = ("x", "y", "node")
    exchange = functools.partial(lax.all_to_all, split_axis=0, concat_axis=0, tiled=True)

    def gather(v):
        return jnp.stack([lax.ppermute(v, "x", [(i, (i + k) % ROW) for i in range(ROW)]) for k in range(1, ROW)])

    ids, scores = expert_ids.T, scores.T
    recv = exchange(pack(ids, scores, grad_out), both)
    hidden = order(hidden_act[0])
    table = jnp.concatenate([scores, ids.astype(f32)], axis=0)
    hidden, far_tokens, far_table = lax.optimization_barrier((hidden, tokens, table))
    others, tables = gather(far_tokens), gather(far_table)
    recv, others, tables = lax.optimization_barrier((recv, others, tables))
    part, slot, rows = expert(recv, hidden, down_weight[0].T)
    slot = exchange(slot, "dp")
    summed = lax.psum_scatter(part, "dp", scatter_dimension=0, tiled=True)
    back = exchange(spread(slot), both)
    weight_grad = lax.dot_general(hidden, rows, (((0,), (0,)), ((), ())), preferred_element_type=f32)
    weight_grad = weight_grad.astype(bf16)[None]
    back, weight_grad = lax.optimization_barrier((back, weight_grad))
    x = lax.axis_index("x").astype(jnp.int32).reshape(1)
    gate_rows = exchange(gate(x, table, tables, back, tokens, others), ("y", "node"))
    gate_row = jnp.sum(gate_rows, axis=0, keepdims=True)
    gate_grad = exchange(jnp.broadcast_to(gate_row, (EXP, FEAT)), both)
    return (weight_grad, summed[None], gate_grad)


def solution(mesh):
    devices = mesh.devices.reshape(ROW, -1, *mesh.devices.shape[1:])
    both = ("x", "y", "node")
    return jax.shard_map(
        body,
        mesh=jax.sharding.Mesh(devices, (*both, "dp")),
        in_specs=(P(both, "dp"), P(both, "dp"), P(both, None), P(both, None), P(both, None, None), P(both, None, "dp")),
        out_specs=(P(both, None, "dp"), P(both, "dp", None), P(None, "dp")),
        check_vma=False,
    )
```

```python
import functools

import jax
import jax.numpy as jnp
from jax import lax
from jax.experimental import pallas as pl
from jax.experimental.pallas import tpu as pltpu
from jax.sharding import PartitionSpec as P

route_scale = 2.5
TOKS = 128
TOP = 8
EXP = 64
MOST = 20
MAIN = 16
EXTRA = MOST - MAIN
FEAT = 896
LANES = 128
COLS = FEAT // LANES
PIECE = COLS * MAIN + 32
HID = 1024
SLOTS = EXP * MOST
GROUPS = 8
BLOCK = SLOTS // GROUPS
ROW = 4
MIB = 1024 * 1024
bf16, f32 = jnp.bfloat16, jnp.float32


def routing(ids, scores):
    expert = lax.broadcasted_iota(jnp.int32, (EXP, TOKS), 0)
    hit = ids[0:1, :] == expert
    for k in range(1, TOP):
        hit = hit | (ids[k : k + 1, :] == expert)
    earlier = (
        lax.broadcasted_iota(jnp.int32, (TOKS, TOKS), 0) < lax.broadcasted_iota(jnp.int32, (TOKS, TOKS), 1)
    )
    ones = jnp.where(hit, 1.0, 0.0)
    rank = jnp.dot(
        ones.astype(bf16), jnp.where(earlier, 1.0, 0.0).astype(bf16), preferred_element_type=f32
    )
    rank = jnp.where(hit, rank, -1.0)
    chosen = jnp.where(hit, scores, 0.0)
    total = jnp.sum(chosen, axis=0, keepdims=True)
    weights = (route_scale * chosen / total).astype(bf16).astype(f32)
    return hit, chosen, total, weights, rank


def pack_kernel(
    ids_any, scores_any, grad_any, send_any, ids_ref, scores_ref, grad_ref, rank_ref, weight_ref, send_ref, sems, out_sems
):
    copies = [
        pltpu.make_async_copy(ids_any, ids_ref, sems.at[0]),
        pltpu.make_async_copy(scores_any, scores_ref, sems.at[1]),
        pltpu.make_async_copy(grad_any, grad_ref, sems.at[2]),
    ]
    for copy in copies:
        copy.start()
    copies[0].wait()
    copies[1].wait()
    _, _, _, weights, rank = routing(ids_ref[...], scores_ref[...])
    rank_ref[...] = rank
    weight_ref[...] = weights
    copies[2].wait()
    grad = grad_ref[...]
    row = lax.broadcasted_iota(jnp.int32, (8, MAIN, TOKS), 1)
    main_rank = row.astype(f32)
    extra_rank = (MAIN + row % EXTRA).astype(f32)
    quarter = lax.broadcasted_iota(jnp.int32, (8 * MAIN, LANES), 0) % MAIN // EXTRA

    outs = []
    for i in range(EXP // 8):
        at = slice(8 * i, 8 * i + 8)
        ranks = rank_ref[at, :][:, None, :]
        gains = weight_ref[at, :][:, None, :]
        place = jnp.where(ranks == main_rank, gains, 0.0).reshape(8 * MAIN, TOKS).astype(bf16)
        rows = jnp.dot(place, grad, preferred_element_type=f32)
        for j in range(COLS):
            send_ref[at, MAIN * j : MAIN * (j + 1), :] = (
                rows[:, LANES * j : LANES * (j + 1)].astype(bf16).reshape(8, MAIN, LANES)
            )
        place = jnp.where(ranks == extra_rank, gains, 0.0).reshape(8 * MAIN, TOKS).astype(bf16)
        rows = jnp.dot(place, grad, preferred_element_type=f32)
        for part in range(2):
            mixed = jnp.zeros((8 * MAIN, LANES), f32)
            for q in range(4):
                j = part * 4 + q
                if j < COLS:
                    mixed = jnp.where(quarter == q, rows[:, LANES * j : LANES * (j + 1)], mixed)
            start = COLS * MAIN + part * MAIN
            send_ref[at, start : start + MAIN, :] = mixed.astype(bf16).reshape(8, MAIN, LANES)
        outs.append(pltpu.make_async_copy(send_ref.at[at], send_any.at[at], out_sems.at[i]))
        outs[i].start()
    for out in outs:
        out.wait()


def pack(ids, scores, grad):
    return pl.pallas_call(
        pack_kernel,
        in_specs=[pl.BlockSpec(memory_space=pl.ANY)] * 3,
        out_specs=pl.BlockSpec(memory_space=pl.ANY),
        out_shape=jax.ShapeDtypeStruct((EXP, PIECE, LANES), bf16),
        scratch_shapes=[
            pltpu.VMEM((TOP, TOKS), jnp.int32),
            pltpu.VMEM((EXP, TOKS), f32),
            pltpu.VMEM((TOKS, FEAT), bf16),
            pltpu.VMEM((EXP, TOKS), f32),
            pltpu.VMEM((EXP, TOKS), f32),
            pltpu.VMEM((EXP, PIECE, LANES), bf16),
            pltpu.SemaphoreType.DMA((3,)),
            pltpu.SemaphoreType.DMA((EXP // 8,)),
        ],
        compiler_params=pltpu.CompilerParams(vmem_limit_bytes=60 * MIB),
        cost_estimate=pl.CostEstimate(flops=500_000_000, bytes_accessed=2_700_000, transcendentals=0),
    )(ids, scores, grad)


def source_order(i):
    e = i - 8 * MAIN
    return jnp.where(i < 8 * MAIN, i // MAIN * MOST + i % MAIN, e // EXTRA * MOST + MAIN + e % EXTRA)


def order_kernel(x_ref, y_ref):
    i = lax.broadcasted_iota(jnp.int32, (BLOCK, BLOCK), 0)
    j = lax.broadcasted_iota(jnp.int32, (BLOCK, BLOCK), 1)
    move = jnp.where(source_order(i) == j, 1.0, 0.0).astype(bf16)
    y_ref[...] = jnp.dot(move, x_ref[...], preferred_element_type=f32).astype(bf16)


def order(hidden):
    return pl.pallas_call(
        order_kernel,
        grid=(GROUPS,),
        in_specs=[pl.BlockSpec((BLOCK, HID), lambda i: (i, 0))],
        out_specs=pl.BlockSpec((BLOCK, HID), lambda i: (i, 0)),
        out_shape=jax.ShapeDtypeStruct((SLOTS, HID), bf16),
        cost_estimate=pl.CostEstimate(flops=500_000_000, bytes_accessed=5_300_000, transcendentals=0),
    )(hidden)


PARTS = 2
CHUNK = SLOTS // PARTS
PAIR = EXP // PARTS
SLOT_ROWS = 16


def expert_kernel(
    recv_any, hidden_any, down_ref, part_any, slot_ref, rows_any,
    recv_ref, hidden_ref, part_ref, rows_ref, in_sems, out_sems,
):
    come, saved, stores = [], [], []
    for c in range(PARTS):
        at = slice(c * PAIR, (c + 1) * PAIR)
        come.append(pltpu.make_async_copy(recv_any.at[at], recv_ref.at[at], in_sems.at[0, c]))
        at = slice(c * CHUNK, (c + 1) * CHUNK)
        saved.append(pltpu.make_async_copy(hidden_any.at[at], hidden_ref.at[at], in_sems.at[1, c]))
        stores.append(
            [
                pltpu.make_async_copy(rows_ref.at[at], rows_any.at[at], out_sems.at[0, c]),
                pltpu.make_async_copy(part_ref.at[at], part_any.at[at], out_sems.at[1, c]),
            ]
        )
    for c in range(PARTS):
        come[c].start()
        saved[c].start()

    i = lax.broadcasted_iota(jnp.int32, (LANES, LANES), 0)
    j = lax.broadcasted_iota(jnp.int32, (LANES, LANES), 1)
    q, source, r = i // 32, i % 32 // EXTRA, i % EXTRA
    move = jnp.where(source * MAIN + q * EXTRA + r == j, 1.0, 0.0).astype(bf16)
    ones = jnp.ones((8, LANES), bf16)
    slot_ref[...] = jnp.zeros_like(slot_ref)
    for c in range(PARTS):
        at = slice(c * CHUNK, (c + 1) * CHUNK)
        come[c].wait()
        for g in range(c * PAIR // 8, (c + 1) * PAIR // 8):
            some = slice(8 * g, 8 * g + 8)
            for j in range(COLS):
                rows_ref[BLOCK * g : BLOCK * g + LANES, LANES * j : LANES * (j + 1)] = recv_ref[
                    some, MAIN * j : MAIN * (j + 1), :
                ].reshape(LANES, LANES)
            for part in range(2):
                start = COLS * MAIN + part * MAIN
                x = recv_ref[some, start : start + MAIN, :].reshape(LANES, LANES)
                y = jnp.dot(move, x, preferred_element_type=f32).astype(bf16)
                for q in range(4):
                    j = part * 4 + q
                    if j < COLS:
                        rows_ref[BLOCK * g + LANES : BLOCK * (g + 1), LANES * j : LANES * (j + 1)] = y[
                            32 * q : 32 * (q + 1)
                        ]
        stores[c][0].start()
        saved[c].wait()
        terms = []
        whole = jnp.dot(rows_ref[at, :], down_ref[...], preferred_element_type=f32)
        for g in range(CHUNK // BLOCK * c, CHUNK // BLOCK * (c + 1)):
            line = slice(BLOCK * g, BLOCK * (g + 1))
            part = whole[BLOCK * g - c * CHUNK : BLOCK * (g + 1) - c * CHUNK]
            both = part * hidden_ref[line, :].astype(f32)
            terms.append(sum(both[:, LANES * q : LANES * (q + 1)] for q in range(HID // LANES)))
            part = jnp.concatenate(
                [
                    part[first + size * s : first + size * (s + 1)]
                    for s in range(8)
                    for first, size in ((0, MAIN), (8 * MAIN, EXTRA))
                ],
                axis=0,
            )
            part_ref[line, :] = part.astype(bf16)
        rest = jnp.concatenate(terms, axis=0)
        stores[c][1].start()
        sums = jnp.zeros((8, CHUNK), f32)
        for _ in range(3):
            term = rest.astype(bf16)
            rest = rest - term.astype(f32)
            sums = sums + lax.dot_general(ones, term, (((1,), (1,)), ((), ())), preferred_element_type=f32)
        for h in range(CHUNK // BLOCK):
            g = CHUNK // BLOCK * c + h
            slot_ref[:, g, :] = sums[:, BLOCK * h : BLOCK * h + LANES]
            slot_ref[:, GROUPS + g, : BLOCK - LANES] = sums[:, BLOCK * h + LANES : BLOCK * (h + 1)]
    for pair in stores:
        for store in pair:
            store.wait()


EXPERT_LIMIT = 52


def expert(recv, hidden, down_t):
    any_space = pl.BlockSpec(memory_space=pl.ANY)
    return pl.pallas_call(
        expert_kernel,
        in_specs=[any_space, any_space, pl.BlockSpec(memory_space=pltpu.VMEM)],
        out_specs=[any_space, pl.BlockSpec(memory_space=pltpu.VMEM), any_space],
        out_shape=[
            jax.ShapeDtypeStruct((SLOTS, HID), bf16),
            jax.ShapeDtypeStruct((GROUPS, SLOT_ROWS, LANES), f32),
            jax.ShapeDtypeStruct((SLOTS, FEAT), bf16),
        ],
        scratch_shapes=[
            pltpu.VMEM((EXP, PIECE, LANES), bf16),
            pltpu.VMEM((SLOTS, HID), bf16),
            pltpu.VMEM((SLOTS, HID), bf16),
            pltpu.VMEM((SLOTS, FEAT), bf16),
            pltpu.SemaphoreType.DMA((2, PARTS)),
            pltpu.SemaphoreType.DMA((2, PARTS)),
        ],
        compiler_params=pltpu.CompilerParams(vmem_limit_bytes=EXPERT_LIMIT * MIB),
        cost_estimate=pl.CostEstimate(flops=2_400_000_000, bytes_accessed=11_000_000, transcendentals=0),
    )(recv, hidden, down_t)


def spread_kernel(slot_ref, out_ref):
    summed = jnp.sum(slot_ref[...], axis=0)
    main = summed[:GROUPS]
    extra = pltpu.roll(summed[GROUPS:], MAIN, 1)
    lane = lax.broadcasted_iota(jnp.int32, (GROUPS, LANES), 1)
    span = lane[:1] // 32
    for place in range(8):
        a = pltpu.roll(main, -MAIN * place % LANES, 1) if place else main
        b = pltpu.roll(extra, -EXTRA * place % LANES, 1) if place else extra
        value = jnp.where(lane < MAIN, a, b)
        moved = [pltpu.roll(value, 32 * k, 1) if k else value for k in range(ROW)]
        for x in range(ROW):
            for high in range(2):
                line = jnp.zeros((1, LANES), f32)
                for k in range(ROW):
                    g = (x - k) % ROW * 2 + high
                    line = jnp.where(span == k, moved[k][g : g + 1], line)
                at = EXP // ROW * x + 8 * high + place
                out_ref[at : at + 1, :] = line


def spread(slot):
    return pl.pallas_call(
        spread_kernel,
        out_shape=jax.ShapeDtypeStruct((EXP, LANES), f32),
        compiler_params=pltpu.CompilerParams(vmem_limit_bytes=2 * MIB),
        cost_estimate=pl.CostEstimate(flops=10_000, bytes_accessed=100_000, transcendentals=0),
    )(slot)


def gate_kernel(x_ref, table_ref, tables_ref, back_ref, tokens_ref, others_ref, out_ref, logit_ref):
    for k in range(ROW):
        table = tables_ref[k - 1] if k else table_ref[...]
        hit, chosen, total, weights, rank = routing(table[EXP:].astype(jnp.int32), table[:EXP])
        route = jnp.zeros((EXP, TOKS), f32)
        for r in range(MOST):
            at = 32 * k + r
            route = route + jnp.where(rank == float(r), back_ref[:, at : at + 1], 0.0)
        route = jnp.where(hit, route / jnp.where(hit, weights, 1.0), 0.0)
        mixed = jnp.sum(route * chosen, axis=0, keepdims=True) / total
        score = route_scale / total * (route - mixed)
        logit_ref[:, TOKS * k : TOKS * (k + 1)] = (score * chosen * (1.0 - chosen)).astype(bf16)
    own = pl.ds(pl.multiple_of(x_ref[0] * (EXP // ROW), EXP // ROW), EXP // ROW)
    grad = jnp.zeros((EXP // ROW, FEAT), f32)
    for k in range(ROW):
        tokens = others_ref[k - 1] if k else tokens_ref[...]
        grad = grad + jnp.dot(logit_ref[own, TOKS * k : TOKS * (k + 1)], tokens, preferred_element_type=f32)
    out_ref[...] = grad


def gate(x, table, tables, back, tokens, others):
    return pl.pallas_call(
        gate_kernel,
        in_specs=[pl.BlockSpec(memory_space=pltpu.SMEM)] + [pl.BlockSpec(memory_space=pltpu.VMEM)] * 5,
        out_shape=jax.ShapeDtypeStruct((EXP // ROW, FEAT), f32),
        scratch_shapes=[pltpu.VMEM((EXP, ROW * TOKS), bf16)],
        compiler_params=pltpu.CompilerParams(vmem_limit_bytes=6 * MIB),
        cost_estimate=pl.CostEstimate(flops=30_000_000, bytes_accessed=1_200_000, transcendentals=0),
    )(x, table, tables, back, tokens, others)


def body(grad_out, tokens, scores, expert_ids, hidden_act, down_weight):
    both = ("x", "y", "node")
    exchange = functools.partial(lax.all_to_all, split_axis=0, concat_axis=0, tiled=True)

    def gather(v):
        return jnp.stack([lax.ppermute(v, "x", [(i, (i + k) % ROW) for i in range(ROW)]) for k in range(1, ROW)])

    ids, scores = expert_ids.T, scores.T
    recv = exchange(pack(ids, scores, grad_out), both)
    hidden = order(hidden_act[0])
    table = jnp.concatenate([scores, ids.astype(f32)], axis=0)
    hidden, far_tokens, far_table = lax.optimization_barrier((hidden, tokens, table))
    others, tables = gather(far_tokens), gather(far_table)
    recv, others, tables = lax.optimization_barrier((recv, others, tables))
    part, slot, rows = expert(recv, hidden, down_weight[0].T)
    slot = exchange(slot, "dp")
    summed = lax.psum_scatter(part, "dp", scatter_dimension=0, tiled=True)
    back = exchange(spread(slot), both)
    weight_grad = lax.dot_general(hidden, rows, (((0,), (0,)), ((), ())), preferred_element_type=f32)
    weight_grad = weight_grad.astype(bf16)[None]
    back, weight_grad = lax.optimization_barrier((back, weight_grad))
    x = lax.axis_index("x").astype(jnp.int32).reshape(1)
    gate_rows = exchange(gate(x, table, tables, back, tokens, others), ("y", "node"))
    gate_row = jnp.sum(gate_rows, axis=0, keepdims=True)
    gate_grad = exchange(jnp.broadcast_to(gate_row, (EXP, FEAT)), both)
    return (weight_grad, summed[None], gate_grad)


def solution(mesh):
    devices = mesh.devices.reshape(ROW, -1, *mesh.devices.shape[1:])
    both = ("x", "y", "node")
    return jax.shard_map(
        body,
        mesh=jax.sharding.Mesh(devices, (*both, "dp")),
        in_specs=(P(both, "dp"), P(both, "dp"), P(both, None), P(both, None), P(both, None, None), P(both, None, "dp")),
        out_specs=(P(both, None, "dp"), P(both, "dp", None), P(None, "dp")),
        check_vma=False,
    )
```

```python
import functools

import jax
import jax.numpy as jnp
from jax import lax
from jax.experimental import pallas as pl
from jax.experimental.pallas import tpu as pltpu
from jax.sharding import PartitionSpec as P

route_scale = 2.5
TOKS = 128
TOP = 8
EXP = 64
MOST = 20
MAIN = 16
EXTRA = MOST - MAIN
FEAT = 896
LANES = 128
COLS = FEAT // LANES
PIECE = COLS * MAIN + 32
HID = 1024
SLOTS = EXP * MOST
GROUPS = 8
BLOCK = SLOTS // GROUPS
ROW = 4
MIB = 1024 * 1024
bf16, f32 = jnp.bfloat16, jnp.float32


def routing(ids, scores):
    expert = lax.broadcasted_iota(jnp.int32, (EXP, TOKS), 0)
    hit = ids[0:1, :] == expert
    for k in range(1, TOP):
        hit = hit | (ids[k : k + 1, :] == expert)
    earlier = (
        lax.broadcasted_iota(jnp.int32, (TOKS, TOKS), 0) < lax.broadcasted_iota(jnp.int32, (TOKS, TOKS), 1)
    )
    ones = jnp.where(hit, 1.0, 0.0)
    rank = jnp.dot(
        ones.astype(bf16), jnp.where(earlier, 1.0, 0.0).astype(bf16), preferred_element_type=f32
    )
    rank = jnp.where(hit, rank, -1.0)
    chosen = jnp.where(hit, scores, 0.0)
    total = jnp.sum(chosen, axis=0, keepdims=True)
    weights = (route_scale * chosen / total).astype(bf16).astype(f32)
    return hit, chosen, total, weights, rank


def pack_kernel(
    ids_any, scores_any, grad_any, send_any, ids_ref, scores_ref, grad_ref, rank_ref, weight_ref, send_ref, sems, out_sems
):
    copies = [
        pltpu.make_async_copy(ids_any, ids_ref, sems.at[0]),
        pltpu.make_async_copy(scores_any, scores_ref, sems.at[1]),
        pltpu.make_async_copy(grad_any, grad_ref, sems.at[2]),
    ]
    for copy in copies:
        copy.start()
    copies[0].wait()
    copies[1].wait()
    _, _, _, weights, rank = routing(ids_ref[...], scores_ref[...])
    rank_ref[...] = rank
    weight_ref[...] = weights
    copies[2].wait()
    grad = grad_ref[...]
    row = lax.broadcasted_iota(jnp.int32, (8, MAIN, TOKS), 1)
    main_rank = row.astype(f32)
    extra_rank = (MAIN + row % EXTRA).astype(f32)
    quarter = lax.broadcasted_iota(jnp.int32, (8 * MAIN, LANES), 0) % MAIN // EXTRA

    outs = []
    for i in range(EXP // 8):
        at = slice(8 * i, 8 * i + 8)
        ranks = rank_ref[at, :][:, None, :]
        gains = weight_ref[at, :][:, None, :]
        place = jnp.where(ranks == main_rank, gains, 0.0).reshape(8 * MAIN, TOKS).astype(bf16)
        rows = jnp.dot(place, grad, preferred_element_type=f32)
        for j in range(COLS):
            send_ref[at, MAIN * j : MAIN * (j + 1), :] = (
                rows[:, LANES * j : LANES * (j + 1)].astype(bf16).reshape(8, MAIN, LANES)
            )
        place = jnp.where(ranks == extra_rank, gains, 0.0).reshape(8 * MAIN, TOKS).astype(bf16)
        rows = jnp.dot(place, grad, preferred_element_type=f32)
        for part in range(2):
            mixed = jnp.zeros((8 * MAIN, LANES), f32)
            for q in range(4):
                j = part * 4 + q
                if j < COLS:
                    mixed = jnp.where(quarter == q, rows[:, LANES * j : LANES * (j + 1)], mixed)
            start = COLS * MAIN + part * MAIN
            send_ref[at, start : start + MAIN, :] = mixed.astype(bf16).reshape(8, MAIN, LANES)
        outs.append(pltpu.make_async_copy(send_ref.at[at], send_any.at[at], out_sems.at[i]))
        outs[i].start()
    for out in outs:
        out.wait()


def pack(ids, scores, grad):
    return pl.pallas_call(
        pack_kernel,
        in_specs=[pl.BlockSpec(memory_space=pl.ANY)] * 3,
        out_specs=pl.BlockSpec(memory_space=pl.ANY),
        out_shape=jax.ShapeDtypeStruct((EXP, PIECE, LANES), bf16),
        scratch_shapes=[
            pltpu.VMEM((TOP, TOKS), jnp.int32),
            pltpu.VMEM((EXP, TOKS), f32),
            pltpu.VMEM((TOKS, FEAT), bf16),
            pltpu.VMEM((EXP, TOKS), f32),
            pltpu.VMEM((EXP, TOKS), f32),
            pltpu.VMEM((EXP, PIECE, LANES), bf16),
            pltpu.SemaphoreType.DMA((3,)),
            pltpu.SemaphoreType.DMA((EXP // 8,)),
        ],
        compiler_params=pltpu.CompilerParams(vmem_limit_bytes=60 * MIB),
        cost_estimate=pl.CostEstimate(flops=500_000_000, bytes_accessed=2_700_000, transcendentals=0),
    )(ids, scores, grad)


def source_order(i):
    e = i - 8 * MAIN
    return jnp.where(i < 8 * MAIN, i // MAIN * MOST + i % MAIN, e // EXTRA * MOST + MAIN + e % EXTRA)


def order_kernel(x_ref, y_ref):
    i = lax.broadcasted_iota(jnp.int32, (BLOCK, BLOCK), 0)
    j = lax.broadcasted_iota(jnp.int32, (BLOCK, BLOCK), 1)
    move = jnp.where(source_order(i) == j, 1.0, 0.0).astype(bf16)
    y_ref[...] = jnp.dot(move, x_ref[...], preferred_element_type=f32).astype(bf16)


def order(hidden):
    return pl.pallas_call(
        order_kernel,
        grid=(GROUPS,),
        in_specs=[pl.BlockSpec((BLOCK, HID), lambda i: (i, 0))],
        out_specs=pl.BlockSpec((BLOCK, HID), lambda i: (i, 0)),
        out_shape=jax.ShapeDtypeStruct((SLOTS, HID), bf16),
        cost_estimate=pl.CostEstimate(flops=500_000_000, bytes_accessed=5_300_000, transcendentals=0),
    )(hidden)


def extra_place(i):
    return i % 32 // EXTRA * MAIN + i // 32 * EXTRA + i % EXTRA


def output_kernel(hidden_ref, down_ref, out_ref):
    y = jnp.dot(hidden_ref[...], down_ref[...], preferred_element_type=f32).astype(bf16)
    j = lax.broadcasted_iota(jnp.int32, (LANES, LANES), 0)
    i = lax.broadcasted_iota(jnp.int32, (LANES, LANES), 1)
    move = jnp.where(extra_place(i) == j, 1.0, 0.0).astype(bf16)
    for j in range(COLS):
        out_ref[:, MAIN * j : MAIN * (j + 1), :] = y[: 8 * MAIN, LANES * j : LANES * (j + 1)].reshape(8, MAIN, LANES)
    for part in range(2):
        blocks = []
        for q in range(4):
            j = part * 4 + q
            empty = jnp.zeros((32, LANES), bf16)
            blocks.append(y[8 * MAIN :, LANES * j : LANES * (j + 1)] if j < COLS else empty)
        x = jnp.dot(move, jnp.concatenate(blocks, axis=0), preferred_element_type=f32).astype(bf16)
        start = COLS * MAIN + part * MAIN
        out_ref[:, start : start + MAIN, :] = x.reshape(8, MAIN, LANES)


def outputs(hidden, down):
    return pl.pallas_call(
        output_kernel,
        grid=(GROUPS,),
        in_specs=[pl.BlockSpec((BLOCK, HID), lambda i: (i, 0)), pl.BlockSpec((HID, FEAT), lambda i: (0, 0))],
        out_specs=pl.BlockSpec((8, PIECE, LANES), lambda i: (i, 0, 0)),
        out_shape=jax.ShapeDtypeStruct((EXP, PIECE, LANES), bf16),
        compiler_params=pltpu.CompilerParams(vmem_limit_bytes=56 * MIB),
        cost_estimate=pl.CostEstimate(flops=2_400_000_000, bytes_accessed=6_900_000, transcendentals=0),
    )(hidden, down)


def slot_kernel(recv_any, outs_any, slot_ref, recv_ref, outs_ref, sems):
    copies = []
    for c in range(PARTS):
        at = slice(c * PAIR, (c + 1) * PAIR)
        copies.append(
            [
                pltpu.make_async_copy(recv_any.at[at], recv_ref.at[at], sems.at[0, c]),
                pltpu.make_async_copy(outs_any.at[at], outs_ref.at[at], sems.at[1, c]),
            ]
        )
        for copy in copies[c]:
            copy.start()
    ones = jnp.ones((8, LANES), bf16)
    for c in range(PARTS):
        at = slice(c * PAIR, (c + 1) * PAIR)
        for copy in copies[c]:
            copy.wait()
        tiles = []
        for j in range(PIECE // MAIN):
            rows = slice(MAIN * j, MAIN * (j + 1))
            tiles.append(recv_ref[at, rows, :].astype(f32) * outs_ref[at, rows, :].astype(f32))
        for kind, some in enumerate((tiles[:COLS], tiles[COLS:])):
            rest = sum(some).reshape(PAIR * MAIN, LANES)
            sums = jnp.zeros((8, PAIR * MAIN), f32)
            for _ in range(3):
                term = rest.astype(bf16)
                rest = rest - term.astype(f32)
                sums = sums + lax.dot_general(ones, term, (((1,), (1,)), ((), ())), preferred_element_type=f32)
            for h in range(PAIR // 8):
                slot_ref[:, kind * GROUPS + PAIR // 8 * c + h, :] = sums[:, LANES * h : LANES * (h + 1)]


def slots(recv, outs):
    any_space = pl.BlockSpec(memory_space=pl.ANY)
    return pl.pallas_call(
        slot_kernel,
        in_specs=[any_space] * 2,
        out_shape=jax.ShapeDtypeStruct((GROUPS, SLOT_ROWS, LANES), f32),
        scratch_shapes=[
            pltpu.VMEM((EXP, PIECE, LANES), bf16),
            pltpu.VMEM((EXP, PIECE, LANES), bf16),
            pltpu.SemaphoreType.DMA((2, PARTS)),
        ],
        compiler_params=pltpu.CompilerParams(vmem_limit_bytes=52 * MIB),
        cost_estimate=pl.CostEstimate(flops=10_000_000, bytes_accessed=4_800_000, transcendentals=0),
    )(recv, outs)


PARTS = 2
CHUNK = SLOTS // PARTS
PAIR = EXP // PARTS
SLOT_ROWS = 16


def expert_kernel(
    recv_any, down_ref, part_any, rows_any, recv_ref, part_ref, rows_ref, in_sems, out_sems,
):
    come, stores = [], []
    for c in range(PARTS):
        at = slice(c * PAIR, (c + 1) * PAIR)
        come.append(pltpu.make_async_copy(recv_any.at[at], recv_ref.at[at], in_sems.at[c]))
        at = slice(c * CHUNK, (c + 1) * CHUNK)
        stores.append(
            [
                pltpu.make_async_copy(rows_ref.at[at], rows_any.at[at], out_sems.at[0, c]),
                pltpu.make_async_copy(part_ref.at[at], part_any.at[at], out_sems.at[1, c]),
            ]
        )
    for c in range(PARTS):
        come[c].start()

    i = lax.broadcasted_iota(jnp.int32, (LANES, LANES), 0)
    j = lax.broadcasted_iota(jnp.int32, (LANES, LANES), 1)
    move = jnp.where(extra_place(i) == j, 1.0, 0.0).astype(bf16)
    for c in range(PARTS):
        at = slice(c * CHUNK, (c + 1) * CHUNK)
        come[c].wait()
        for g in range(c * PAIR // 8, (c + 1) * PAIR // 8):
            some = slice(8 * g, 8 * g + 8)
            for j in range(COLS):
                rows_ref[BLOCK * g : BLOCK * g + LANES, LANES * j : LANES * (j + 1)] = recv_ref[
                    some, MAIN * j : MAIN * (j + 1), :
                ].reshape(LANES, LANES)
            for part in range(2):
                start = COLS * MAIN + part * MAIN
                x = recv_ref[some, start : start + MAIN, :].reshape(LANES, LANES)
                y = jnp.dot(move, x, preferred_element_type=f32).astype(bf16)
                for q in range(4):
                    j = part * 4 + q
                    if j < COLS:
                        rows_ref[BLOCK * g + LANES : BLOCK * (g + 1), LANES * j : LANES * (j + 1)] = y[
                            32 * q : 32 * (q + 1)
                        ]
        stores[c][0].start()
        whole = jnp.dot(rows_ref[at, :], down_ref[...], preferred_element_type=f32)
        for g in range(CHUNK // BLOCK * c, CHUNK // BLOCK * (c + 1)):
            line = slice(BLOCK * g, BLOCK * (g + 1))
            part = whole[BLOCK * g - c * CHUNK : BLOCK * (g + 1) - c * CHUNK]
            part = jnp.concatenate(
                [
                    part[first + size * s : first + size * (s + 1)]
                    for s in range(8)
                    for first, size in ((0, MAIN), (8 * MAIN, EXTRA))
                ],
                axis=0,
            )
            part_ref[line, :] = part.astype(bf16)
        stores[c][1].start()
    for pair in stores:
        for store in pair:
            store.wait()


EXPERT_LIMIT = 52


def expert(recv, down_t):
    any_space = pl.BlockSpec(memory_space=pl.ANY)
    return pl.pallas_call(
        expert_kernel,
        in_specs=[any_space, pl.BlockSpec(memory_space=pltpu.VMEM)],
        out_specs=[any_space, any_space],
        out_shape=[
            jax.ShapeDtypeStruct((SLOTS, HID), bf16),
            jax.ShapeDtypeStruct((SLOTS, FEAT), bf16),
        ],
        scratch_shapes=[
            pltpu.VMEM((EXP, PIECE, LANES), bf16),
            pltpu.VMEM((SLOTS, HID), bf16),
            pltpu.VMEM((SLOTS, FEAT), bf16),
            pltpu.SemaphoreType.DMA((PARTS,)),
            pltpu.SemaphoreType.DMA((2, PARTS)),
        ],
        compiler_params=pltpu.CompilerParams(vmem_limit_bytes=EXPERT_LIMIT * MIB),
        cost_estimate=pl.CostEstimate(flops=2_400_000_000, bytes_accessed=11_000_000, transcendentals=0),
    )(recv, down_t)


def spread_kernel(slot_ref, out_ref):
    summed = jnp.sum(slot_ref[...], axis=0)
    main = summed[:GROUPS]
    extra = summed[GROUPS:]
    extra = sum(pltpu.roll(extra, (MAIN - EXTRA * q) % LANES, 1) for q in range(4))
    lane = lax.broadcasted_iota(jnp.int32, (GROUPS, LANES), 1)
    span = lane[:1] // 32
    for place in range(8):
        a = pltpu.roll(main, -MAIN * place % LANES, 1) if place else main
        b = pltpu.roll(extra, -MAIN * place % LANES, 1) if place else extra
        value = jnp.where(lane < MAIN, a, b)
        moved = [pltpu.roll(value, 32 * k, 1) if k else value for k in range(ROW)]
        for x in range(ROW):
            for high in range(2):
                line = jnp.zeros((1, LANES), f32)
                for k in range(ROW):
                    g = (x - k) % ROW * 2 + high
                    line = jnp.where(span == k, moved[k][g : g + 1], line)
                at = EXP // ROW * x + 8 * high + place
                out_ref[at : at + 1, :] = line


def spread(slot):
    return pl.pallas_call(
        spread_kernel,
        out_shape=jax.ShapeDtypeStruct((EXP, LANES), f32),
        compiler_params=pltpu.CompilerParams(vmem_limit_bytes=2 * MIB),
        cost_estimate=pl.CostEstimate(flops=10_000, bytes_accessed=100_000, transcendentals=0),
    )(slot)


def gate_kernel(x_ref, table_ref, tables_ref, back_ref, tokens_ref, others_ref, out_ref, logit_ref):
    for k in range(ROW):
        table = tables_ref[k - 1] if k else table_ref[...]
        hit, chosen, total, weights, rank = routing(table[EXP:].astype(jnp.int32), table[:EXP])
        route = jnp.zeros((EXP, TOKS), f32)
        for r in range(MOST):
            at = 32 * k + r
            route = route + jnp.where(rank == float(r), back_ref[:, at : at + 1], 0.0)
        route = jnp.where(hit, route / jnp.where(hit, weights, 1.0), 0.0)
        mixed = jnp.sum(route * chosen, axis=0, keepdims=True) / total
        score = route_scale / total * (route - mixed)
        logit_ref[:, TOKS * k : TOKS * (k + 1)] = (score * chosen * (1.0 - chosen)).astype(bf16)
    own = pl.ds(pl.multiple_of(x_ref[0] * (EXP // ROW), EXP // ROW), EXP // ROW)
    grad = jnp.zeros((EXP // ROW, FEAT), f32)
    for k in range(ROW):
        tokens = others_ref[k - 1] if k else tokens_ref[...]
        grad = grad + jnp.dot(logit_ref[own, TOKS * k : TOKS * (k + 1)], tokens, preferred_element_type=f32)
    out_ref[...] = grad


def gate(x, table, tables, back, tokens, others):
    return pl.pallas_call(
        gate_kernel,
        in_specs=[pl.BlockSpec(memory_space=pltpu.SMEM)] + [pl.BlockSpec(memory_space=pltpu.VMEM)] * 5,
        out_shape=jax.ShapeDtypeStruct((EXP // ROW, FEAT), f32),
        scratch_shapes=[pltpu.VMEM((EXP, ROW * TOKS), bf16)],
        compiler_params=pltpu.CompilerParams(vmem_limit_bytes=6 * MIB),
        cost_estimate=pl.CostEstimate(flops=30_000_000, bytes_accessed=1_200_000, transcendentals=0),
    )(x, table, tables, back, tokens, others)


def body(grad_out, tokens, scores, expert_ids, hidden_act, down_weight):
    both = ("x", "y", "node")
    exchange = functools.partial(lax.all_to_all, split_axis=0, concat_axis=0, tiled=True)

    def gather(v):
        return jnp.stack([lax.ppermute(v, "x", [(i, (i + k) % ROW) for i in range(ROW)]) for k in range(1, ROW)])

    ids, scores = expert_ids.T, scores.T
    recv = exchange(pack(ids, scores, grad_out), both)
    hidden = order(hidden_act[0])
    table = jnp.concatenate([scores, ids.astype(f32)], axis=0)
    hidden, far_tokens, far_table = lax.optimization_barrier((hidden, tokens, table))
    others, tables = gather(far_tokens), gather(far_table)
    outs = outputs(hidden, down_weight[0])
    recv, others, tables, outs = lax.optimization_barrier((recv, others, tables, outs))
    slot = slots(recv, outs)
    part, rows = expert(recv, down_weight[0].T)
    slot = exchange(slot, "dp")
    part, slot = lax.optimization_barrier((part, slot))
    summed = lax.psum_scatter(part, "dp", scatter_dimension=0, tiled=True)
    back = exchange(spread(slot), both)
    weight_grad = lax.dot_general(hidden, rows, (((0,), (0,)), ((), ())), preferred_element_type=f32)
    weight_grad = weight_grad.astype(bf16)[None]
    back, weight_grad = lax.optimization_barrier((back, weight_grad))
    x = lax.axis_index("x").astype(jnp.int32).reshape(1)
    gate_rows = exchange(gate(x, table, tables, back, tokens, others), ("y", "node"))
    gate_row = jnp.sum(gate_rows, axis=0, keepdims=True)
    gate_grad = exchange(jnp.broadcast_to(gate_row, (EXP, FEAT)), both)
    return (weight_grad, summed[None], gate_grad)


def solution(mesh):
    devices = mesh.devices.reshape(ROW, -1, *mesh.devices.shape[1:])
    both = ("x", "y", "node")
    return jax.shard_map(
        body,
        mesh=jax.sharding.Mesh(devices, (*both, "dp")),
        in_specs=(P(both, "dp"), P(both, "dp"), P(both, None), P(both, None), P(both, None, None), P(both, None, "dp")),
        out_specs=(P(both, None, "dp"), P(both, "dp", None), P(None, "dp")),
        check_vma=False,
    )
```

```python
import functools

import jax
import jax.numpy as jnp
from jax import lax
from jax.experimental import pallas as pl
from jax.experimental.pallas import tpu as pltpu
from jax.sharding import PartitionSpec as P

route_scale = 2.5
TOKS = 128
TOP = 8
EXP = 64
MOST = 20
MAIN = 16
EXTRA = MOST - MAIN
FEAT = 896
LANES = 128
COLS = FEAT // LANES
PIECE = COLS * MAIN + 32
HID = 1024
SLOTS = EXP * MOST
GROUPS = 8
BLOCK = SLOTS // GROUPS
ROW = 4
MIB = 1024 * 1024
bf16, f32 = jnp.bfloat16, jnp.float32


def routing(ids, scores):
    expert = lax.broadcasted_iota(jnp.int32, (EXP, TOKS), 0)
    hit = ids[0:1, :] == expert
    for k in range(1, TOP):
        hit = hit | (ids[k : k + 1, :] == expert)
    earlier = (
        lax.broadcasted_iota(jnp.int32, (TOKS, TOKS), 0) < lax.broadcasted_iota(jnp.int32, (TOKS, TOKS), 1)
    )
    ones = jnp.where(hit, 1.0, 0.0)
    rank = jnp.dot(
        ones.astype(bf16), jnp.where(earlier, 1.0, 0.0).astype(bf16), preferred_element_type=f32
    )
    rank = jnp.where(hit, rank, -1.0)
    chosen = jnp.where(hit, scores, 0.0)
    total = jnp.sum(chosen, axis=0, keepdims=True)
    weights = (route_scale * chosen / total).astype(bf16).astype(f32)
    return hit, chosen, total, weights, rank


def pack_kernel(
    ids_any, scores_any, grad_any, send_any, ids_ref, scores_ref, grad_ref, rank_ref, weight_ref, send_ref, sems, out_sems
):
    copies = [
        pltpu.make_async_copy(ids_any, ids_ref, sems.at[0]),
        pltpu.make_async_copy(scores_any, scores_ref, sems.at[1]),
        pltpu.make_async_copy(grad_any, grad_ref, sems.at[2]),
    ]
    for copy in copies:
        copy.start()
    copies[0].wait()
    copies[1].wait()
    _, _, _, weights, rank = routing(ids_ref[...], scores_ref[...])
    rank_ref[...] = rank
    weight_ref[...] = weights
    copies[2].wait()
    grad = grad_ref[...]
    row = lax.broadcasted_iota(jnp.int32, (8, MAIN, TOKS), 1)
    main_rank = row.astype(f32)
    extra_rank = (MAIN + row % EXTRA).astype(f32)
    quarter = lax.broadcasted_iota(jnp.int32, (8 * MAIN, LANES), 0) % MAIN // EXTRA

    outs = []
    for i in range(EXP // 8):
        at = slice(8 * i, 8 * i + 8)
        ranks = rank_ref[at, :][:, None, :]
        gains = weight_ref[at, :][:, None, :]
        place = jnp.where(ranks == main_rank, gains, 0.0).reshape(8 * MAIN, TOKS).astype(bf16)
        rows = jnp.dot(place, grad, preferred_element_type=f32)
        for j in range(COLS):
            send_ref[at, MAIN * j : MAIN * (j + 1), :] = (
                rows[:, LANES * j : LANES * (j + 1)].astype(bf16).reshape(8, MAIN, LANES)
            )
        place = jnp.where(ranks == extra_rank, gains, 0.0).reshape(8 * MAIN, TOKS).astype(bf16)
        rows = jnp.dot(place, grad, preferred_element_type=f32)
        for part in range(2):
            mixed = jnp.zeros((8 * MAIN, LANES), f32)
            for q in range(4):
                j = part * 4 + q
                if j < COLS:
                    mixed = jnp.where(quarter == q, rows[:, LANES * j : LANES * (j + 1)], mixed)
            start = COLS * MAIN + part * MAIN
            send_ref[at, start : start + MAIN, :] = mixed.astype(bf16).reshape(8, MAIN, LANES)
        outs.append(pltpu.make_async_copy(send_ref.at[at], send_any.at[at], out_sems.at[i]))
        outs[i].start()
    for out in outs:
        out.wait()


def pack(ids, scores, grad):
    return pl.pallas_call(
        pack_kernel,
        in_specs=[pl.BlockSpec(memory_space=pl.ANY)] * 3,
        out_specs=pl.BlockSpec(memory_space=pl.ANY),
        out_shape=jax.ShapeDtypeStruct((EXP, PIECE, LANES), bf16),
        scratch_shapes=[
            pltpu.VMEM((TOP, TOKS), jnp.int32),
            pltpu.VMEM((EXP, TOKS), f32),
            pltpu.VMEM((TOKS, FEAT), bf16),
            pltpu.VMEM((EXP, TOKS), f32),
            pltpu.VMEM((EXP, TOKS), f32),
            pltpu.VMEM((EXP, PIECE, LANES), bf16),
            pltpu.SemaphoreType.DMA((3,)),
            pltpu.SemaphoreType.DMA((EXP // 8,)),
        ],
        compiler_params=pltpu.CompilerParams(vmem_limit_bytes=60 * MIB),
        cost_estimate=pl.CostEstimate(flops=500_000_000, bytes_accessed=2_700_000, transcendentals=0),
    )(ids, scores, grad)


def source_order(i):
    e = i - 8 * MAIN
    return jnp.where(i < 8 * MAIN, i // MAIN * MOST + i % MAIN, e // EXTRA * MOST + MAIN + e % EXTRA)


def order_kernel(x_ref, y_ref):
    i = lax.broadcasted_iota(jnp.int32, (BLOCK, BLOCK), 0)
    j = lax.broadcasted_iota(jnp.int32, (BLOCK, BLOCK), 1)
    move = jnp.where(source_order(i) == j, 1.0, 0.0).astype(bf16)
    y_ref[...] = jnp.dot(move, x_ref[...], preferred_element_type=f32).astype(bf16)


def order(hidden):
    return pl.pallas_call(
        order_kernel,
        grid=(GROUPS,),
        in_specs=[pl.BlockSpec((BLOCK, HID), lambda i: (i, 0))],
        out_specs=pl.BlockSpec((BLOCK, HID), lambda i: (i, 0)),
        out_shape=jax.ShapeDtypeStruct((SLOTS, HID), bf16),
        cost_estimate=pl.CostEstimate(flops=500_000_000, bytes_accessed=5_300_000, transcendentals=0),
    )(hidden)


def extra_place(i):
    return i % 32 // EXTRA * MAIN + i // 32 * EXTRA + i % EXTRA


def output_kernel(hidden_ref, down_ref, out_ref):
    y = jnp.dot(hidden_ref[...], down_ref[...], preferred_element_type=f32).astype(bf16)
    j = lax.broadcasted_iota(jnp.int32, (LANES, LANES), 0)
    i = lax.broadcasted_iota(jnp.int32, (LANES, LANES), 1)
    move = jnp.where(extra_place(i) == j, 1.0, 0.0).astype(bf16)
    for j in range(COLS):
        out_ref[:, MAIN * j : MAIN * (j + 1), :] = y[: 8 * MAIN, LANES * j : LANES * (j + 1)].reshape(8, MAIN, LANES)
    for part in range(2):
        blocks = []
        for q in range(4):
            j = part * 4 + q
            empty = jnp.zeros((32, LANES), bf16)
            blocks.append(y[8 * MAIN :, LANES * j : LANES * (j + 1)] if j < COLS else empty)
        x = jnp.dot(move, jnp.concatenate(blocks, axis=0), preferred_element_type=f32).astype(bf16)
        start = COLS * MAIN + part * MAIN
        out_ref[:, start : start + MAIN, :] = x.reshape(8, MAIN, LANES)


def outputs(hidden, down):
    return pl.pallas_call(
        output_kernel,
        grid=(GROUPS,),
        in_specs=[pl.BlockSpec((BLOCK, HID), lambda i: (i, 0)), pl.BlockSpec((HID, FEAT), lambda i: (0, 0))],
        out_specs=pl.BlockSpec((8, PIECE, LANES), lambda i: (i, 0, 0)),
        out_shape=jax.ShapeDtypeStruct((EXP, PIECE, LANES), bf16),
        compiler_params=pltpu.CompilerParams(vmem_limit_bytes=56 * MIB),
        cost_estimate=pl.CostEstimate(flops=2_400_000_000, bytes_accessed=6_900_000, transcendentals=0),
    )(hidden, down)


SLOT_PARTS = 4
SOURCES = EXP // SLOT_PARTS


def slot_kernel(recv_any, outs_any, slot_ref, recv_ref, outs_ref, sems):
    copies = []
    for c in range(SLOT_PARTS):
        at = slice(c * SOURCES, (c + 1) * SOURCES)
        copies.append(
            [
                pltpu.make_async_copy(recv_any.at[at], recv_ref.at[at], sems.at[0, c]),
                pltpu.make_async_copy(outs_any.at[at], outs_ref.at[at], sems.at[1, c]),
            ]
        )
        for copy in copies[c]:
            copy.start()
    ones = jnp.ones((8, LANES), bf16)
    for c in range(SLOT_PARTS):
        at = slice(c * SOURCES, (c + 1) * SOURCES)
        for copy in copies[c]:
            copy.wait()
        tiles = []
        for j in range(PIECE // MAIN):
            rows = slice(MAIN * j, MAIN * (j + 1))
            tiles.append(recv_ref[at, rows, :].astype(f32) * outs_ref[at, rows, :].astype(f32))
        for kind, some in enumerate((tiles[:COLS], tiles[COLS:])):
            rest = sum(some).reshape(SOURCES * MAIN, LANES)
            sums = jnp.zeros((8, SOURCES * MAIN), f32)
            for _ in range(3):
                term = rest.astype(bf16)
                rest = rest - term.astype(f32)
                sums = sums + lax.dot_general(ones, term, (((1,), (1,)), ((), ())), preferred_element_type=f32)
            for h in range(SOURCES // 8):
                slot_ref[:, kind * GROUPS + SOURCES // 8 * c + h, :] = sums[:, LANES * h : LANES * (h + 1)]


def slots(recv, outs):
    any_space = pl.BlockSpec(memory_space=pl.ANY)
    return pl.pallas_call(
        slot_kernel,
        in_specs=[any_space] * 2,
        out_shape=jax.ShapeDtypeStruct((GROUPS, SLOT_ROWS, LANES), f32),
        scratch_shapes=[
            pltpu.VMEM((EXP, PIECE, LANES), bf16),
            pltpu.VMEM((EXP, PIECE, LANES), bf16),
            pltpu.SemaphoreType.DMA((2, SLOT_PARTS)),
        ],
        compiler_params=pltpu.CompilerParams(vmem_limit_bytes=52 * MIB),
        cost_estimate=pl.CostEstimate(flops=10_000_000, bytes_accessed=4_800_000, transcendentals=0),
    )(recv, outs)


PARTS = 2
CHUNK = SLOTS // PARTS
PAIR = EXP // PARTS
SLOT_ROWS = 16


def expert_kernel(
    recv_any, down_ref, part_any, rows_any, recv_ref, part_ref, rows_ref, in_sems, out_sems,
):
    come, stores = [], []
    for c in range(PARTS):
        at = slice(c * PAIR, (c + 1) * PAIR)
        come.append(pltpu.make_async_copy(recv_any.at[at], recv_ref.at[at], in_sems.at[c]))
        at = slice(c * CHUNK, (c + 1) * CHUNK)
        stores.append(
            [
                pltpu.make_async_copy(rows_ref.at[at], rows_any.at[at], out_sems.at[0, c]),
                pltpu.make_async_copy(part_ref.at[at], part_any.at[at], out_sems.at[1, c]),
            ]
        )
    for c in range(PARTS):
        come[c].start()

    i = lax.broadcasted_iota(jnp.int32, (LANES, LANES), 0)
    j = lax.broadcasted_iota(jnp.int32, (LANES, LANES), 1)
    move = jnp.where(extra_place(i) == j, 1.0, 0.0).astype(bf16)
    for c in range(PARTS):
        at = slice(c * CHUNK, (c + 1) * CHUNK)
        come[c].wait()
        for g in range(c * PAIR // 8, (c + 1) * PAIR // 8):
            some = slice(8 * g, 8 * g + 8)
            for j in range(COLS):
                rows_ref[BLOCK * g : BLOCK * g + LANES, LANES * j : LANES * (j + 1)] = recv_ref[
                    some, MAIN * j : MAIN * (j + 1), :
                ].reshape(LANES, LANES)
            for part in range(2):
                start = COLS * MAIN + part * MAIN
                x = recv_ref[some, start : start + MAIN, :].reshape(LANES, LANES)
                y = jnp.dot(move, x, preferred_element_type=f32).astype(bf16)
                for q in range(4):
                    j = part * 4 + q
                    if j < COLS:
                        rows_ref[BLOCK * g + LANES : BLOCK * (g + 1), LANES * j : LANES * (j + 1)] = y[
                            32 * q : 32 * (q + 1)
                        ]
        stores[c][0].start()
        whole = jnp.dot(rows_ref[at, :], down_ref[...], preferred_element_type=f32)
        for g in range(CHUNK // BLOCK * c, CHUNK // BLOCK * (c + 1)):
            line = slice(BLOCK * g, BLOCK * (g + 1))
            part = whole[BLOCK * g - c * CHUNK : BLOCK * (g + 1) - c * CHUNK]
            part = jnp.concatenate(
                [
                    part[first + size * s : first + size * (s + 1)]
                    for s in range(8)
                    for first, size in ((0, MAIN), (8 * MAIN, EXTRA))
                ],
                axis=0,
            )
            part_ref[line, :] = part.astype(bf16)
        stores[c][1].start()
    for pair in stores:
        for store in pair:
            store.wait()


EXPERT_LIMIT = 52


def expert(recv, down_t):
    any_space = pl.BlockSpec(memory_space=pl.ANY)
    return pl.pallas_call(
        expert_kernel,
        in_specs=[any_space, pl.BlockSpec(memory_space=pltpu.VMEM)],
        out_specs=[any_space, any_space],
        out_shape=[
            jax.ShapeDtypeStruct((SLOTS, HID), bf16),
            jax.ShapeDtypeStruct((SLOTS, FEAT), bf16),
        ],
        scratch_shapes=[
            pltpu.VMEM((EXP, PIECE, LANES), bf16),
            pltpu.VMEM((SLOTS, HID), bf16),
            pltpu.VMEM((SLOTS, FEAT), bf16),
            pltpu.SemaphoreType.DMA((PARTS,)),
            pltpu.SemaphoreType.DMA((2, PARTS)),
        ],
        compiler_params=pltpu.CompilerParams(vmem_limit_bytes=EXPERT_LIMIT * MIB),
        cost_estimate=pl.CostEstimate(flops=2_400_000_000, bytes_accessed=11_000_000, transcendentals=0),
    )(recv, down_t)


def spread_kernel(slot_ref, out_ref):
    summed = jnp.sum(slot_ref[...], axis=0)
    main = summed[:GROUPS]
    extra = summed[GROUPS:]
    extra = sum(pltpu.roll(extra, (MAIN - EXTRA * q) % LANES, 1) for q in range(4))
    lane = lax.broadcasted_iota(jnp.int32, (GROUPS, LANES), 1)
    span = lane[:1] // 32
    for place in range(8):
        a = pltpu.roll(main, -MAIN * place % LANES, 1) if place else main
        b = pltpu.roll(extra, -MAIN * place % LANES, 1) if place else extra
        value = jnp.where(lane < MAIN, a, b)
        moved = [pltpu.roll(value, 32 * k, 1) if k else value for k in range(ROW)]
        for x in range(ROW):
            for high in range(2):
                line = jnp.zeros((1, LANES), f32)
                for k in range(ROW):
                    g = (x - k) % ROW * 2 + high
                    line = jnp.where(span == k, moved[k][g : g + 1], line)
                at = EXP // ROW * x + 8 * high + place
                out_ref[at : at + 1, :] = line


def spread(slot):
    return pl.pallas_call(
        spread_kernel,
        out_shape=jax.ShapeDtypeStruct((EXP, LANES), f32),
        compiler_params=pltpu.CompilerParams(vmem_limit_bytes=2 * MIB),
        cost_estimate=pl.CostEstimate(flops=10_000, bytes_accessed=100_000, transcendentals=0),
    )(slot)


def gate_kernel(x_ref, table_ref, tables_ref, back_ref, tokens_ref, others_ref, out_ref, logit_ref):
    for k in range(ROW):
        table = tables_ref[k - 1] if k else table_ref[...]
        hit, chosen, total, weights, rank = routing(table[EXP:].astype(jnp.int32), table[:EXP])
        route = jnp.zeros((EXP, TOKS), f32)
        for r in range(MOST):
            at = 32 * k + r
            route = route + jnp.where(rank == float(r), back_ref[:, at : at + 1], 0.0)
        route = jnp.where(hit, route / jnp.where(hit, weights, 1.0), 0.0)
        mixed = jnp.sum(route * chosen, axis=0, keepdims=True) / total
        score = route_scale / total * (route - mixed)
        logit_ref[:, TOKS * k : TOKS * (k + 1)] = (score * chosen * (1.0 - chosen)).astype(bf16)
    own = pl.ds(pl.multiple_of(x_ref[0] * (EXP // ROW), EXP // ROW), EXP // ROW)
    grad = jnp.zeros((EXP // ROW, FEAT), f32)
    for k in range(ROW):
        tokens = others_ref[k - 1] if k else tokens_ref[...]
        grad = grad + jnp.dot(logit_ref[own, TOKS * k : TOKS * (k + 1)], tokens, preferred_element_type=f32)
    out_ref[...] = grad


def gate(x, table, tables, back, tokens, others):
    return pl.pallas_call(
        gate_kernel,
        in_specs=[pl.BlockSpec(memory_space=pltpu.SMEM)] + [pl.BlockSpec(memory_space=pltpu.VMEM)] * 5,
        out_shape=jax.ShapeDtypeStruct((EXP // ROW, FEAT), f32),
        scratch_shapes=[pltpu.VMEM((EXP, ROW * TOKS), bf16)],
        compiler_params=pltpu.CompilerParams(vmem_limit_bytes=6 * MIB),
        cost_estimate=pl.CostEstimate(flops=30_000_000, bytes_accessed=1_200_000, transcendentals=0),
    )(x, table, tables, back, tokens, others)


def body(grad_out, tokens, scores, expert_ids, hidden_act, down_weight):
    both = ("x", "y", "node")
    exchange = functools.partial(lax.all_to_all, split_axis=0, concat_axis=0, tiled=True)

    def gather(v):
        return jnp.stack([lax.ppermute(v, "x", [(i, (i + k) % ROW) for i in range(ROW)]) for k in range(1, ROW)])

    ids, scores = expert_ids.T, scores.T
    recv = exchange(pack(ids, scores, grad_out), both)
    hidden = order(hidden_act[0])
    table = jnp.concatenate([scores, ids.astype(f32)], axis=0)
    hidden, far_tokens, far_table = lax.optimization_barrier((hidden, tokens, table))
    others, tables = gather(far_tokens), gather(far_table)
    outs = outputs(hidden, down_weight[0])
    recv, others, tables, outs = lax.optimization_barrier((recv, others, tables, outs))
    slot = slots(recv, outs)
    part, rows = expert(recv, down_weight[0].T)
    slot = exchange(slot, "dp")
    part, slot = lax.optimization_barrier((part, slot))
    summed = lax.psum_scatter(part, "dp", scatter_dimension=0, tiled=True)
    back = exchange(spread(slot), both)
    weight_grad = lax.dot_general(hidden, rows, (((0,), (0,)), ((), ())), preferred_element_type=f32)
    weight_grad = weight_grad.astype(bf16)[None]
    back, weight_grad = lax.optimization_barrier((back, weight_grad))
    x = lax.axis_index("x").astype(jnp.int32).reshape(1)
    gate_rows = exchange(gate(x, table, tables, back, tokens, others), ("y", "node"))
    gate_row = jnp.sum(gate_rows, axis=0, keepdims=True)
    gate_grad = exchange(jnp.broadcast_to(gate_row, (EXP, FEAT)), both)
    return (weight_grad, summed[None], gate_grad)


def solution(mesh):
    devices = mesh.devices.reshape(ROW, -1, *mesh.devices.shape[1:])
    both = ("x", "y", "node")
    return jax.shard_map(
        body,
        mesh=jax.sharding.Mesh(devices, (*both, "dp")),
        in_specs=(P(both, "dp"), P(both, "dp"), P(both, None), P(both, None), P(both, None, None), P(both, None, "dp")),
        out_specs=(P(both, None, "dp"), P(both, "dp", None), P(None, "dp")),
        check_vma=False,
    )
```
